32 devices in a mesh: tm: 16 (over z, y, core), space: 2 (over x).
Axes of the slice: x: 2, y: 2, z: 4, core: 2. Of those that a mesh axis runs over, the one named last changes fastest.
Arguments:
- start_states: float32 [16, 64, 256], P('tm', 'space'), may hold values from -6 to 6
- region_map: int32 [64, 256], P('space'), may hold values from 0 to 3
- source: float32 [2, 64, 256], P(None, 'space'), may hold values from -6 to 6
- front: int32 [], replicated, may hold values from 9 to 15
Outputs:
- new_states: float32 [16, 64, 256], P('tm', 'space')
- jumps: float32 [16, 64, 256], P('tm', 'space')
The draws below stay inside these ranges and needn't reach their ends.
All inputs are finite; a program needn't handle non-finite values.
Results may differ from the reference program's by a relative error of at most 0.000027.
Values sent between devices are 32-bit elements; how exact they have to be, the bound alone decides.
A program may use at most 64 MiB of HBM per device.

```python
import math
import jax
import jax.numpy as jnp
from jax import lax

NC = 256
FINE = 16
ITERS = 2
SLICES = 16
NR = 64


def place_ends(array, own_key, smallest, high):
    place = [jax.random.randint(jax.random.fold_in(own_key, axis), (), 0, length) for axis, length in enumerate(array.shape)]
    longest = array.shape.index(max(array.shape))
    neighbour = place[:longest] + [(place[longest] + 1) % array.shape[longest]] + place[longest + 1:]
    return array.at[tuple(place)].set(smallest).at[tuple(neighbour)].set(high)


def shard_levels(own_key, dims, split, smallest, top_value):
    factor_of = 1.0
    for position, shards_of in split:
        draws = jax.random.uniform(jax.random.fold_in(jax.random.fold_in(own_key, 6), position), (shards_of,), jnp.float32, smallest / len(split), top_value / len(split))
        factor_of = factor_of * jnp.repeat(jnp.exp(draws), dims[position] // shards_of).reshape((-1,) + (1,) * (len(dims) - 1 - position))
    return factor_of


def noise(stream_key, dims, width, reach, split=(), kind=jnp.bfloat16):
    drawn = width * jax.random.normal(stream_key, dims, jnp.float32)
    if split:
        drawn = drawn * shard_levels(stream_key, dims, split, -0.22, 0.18)
    return jnp.clip(drawn, -reach, reach).astype(kind)


def setup_inputs(seed: int = 0) -> dict:
    key_of = jax.random.split(jax.random.key(seed), 5)
    return {
        "start_states": noise(key_of[0], (SLICES, NR, NC), 1.0, 6.0, ((0, 16), (1, 2)), jnp.float32),
        "region_map": place_ends(jax.random.randint(key_of[1], (NR, NC), 0, 4), jax.random.fold_in(key_of[1], 1), 0, 3).astype(jnp.int32),
        "source": noise(key_of[2], (2, NR, NC), 1.0, 6.0, ((1, 2),), jnp.float32),
        "front": jax.random.randint(key_of[3], (), SLICES // 2 + 1, SLICES).astype(jnp.int32),
    }


RELUCTIVITY = (1.0, 0.3, 1.0, 0.25)
SATURATION = (0.0, 2.0, 0.0, 1.5)
MOBILITY = (0.15, 0.02, 0.0004, 0.0008)


def lookup(region_map, table):
    result = jnp.zeros(region_map.shape, jnp.float32)
    for region, entry_value in enumerate(table):
        result = result + jnp.where(region_map == region, jnp.float32(entry_value), jnp.float32(0.0))
    return result


def flux_terms(extended, reluctivity, saturation):
    field_cols = jnp.pad(extended, ((0, 0), (1, 1)))
    relu_cols = jnp.pad(reluctivity, ((0, 0), (1, 1)))
    satu_cols = jnp.pad(saturation, ((0, 0), (1, 1)))
    center = field_cols[1:-1, 1:-1]
    own_rel = relu_cols[1:-1, 1:-1]
    own_sat = satu_cols[1:-1, 1:-1]
    divergence = jnp.zeros_like(center)
    diagonal = jnp.zeros_like(center)
    for row_part, col_part in ((slice(0, -2), slice(1, -1)), (slice(2, None), slice(1, -1)), (slice(1, -1), slice(0, -2)), (slice(1, -1), slice(2, None))):
        difference = field_cols[row_part, col_part] - center
        square = difference * difference
        face_rel = 0.5 * (own_rel + relu_cols[row_part, col_part])
        face_sat = 0.5 * (own_sat + satu_cols[row_part, col_part])
        weight = face_rel * (1.0 + face_sat * square / (1.0 + square))
        divergence = divergence + weight * difference
        diagonal = diagonal + weight
    return divergence, diagonal


def compose_maps(earlier, later):
    return (later[0] * earlier[0], later[0] * earlier[1] + later[1])


def reference(start_states, region_map, source, front):
    reluct = lookup(region_map, RELUCTIVITY)
    satur = lookup(region_map, SATURATION)
    mobile = lookup(region_map, MOBILITY)
    padded_rel = jnp.pad(reluct, ((1, 1), (0, 0)))
    padded_sat = jnp.pad(satur, ((1, 1), (0, 0)))
    scale = 2.0 * math.pi / (SLICES * FINE)

    def fine_solve(inputs):
        field_now, slice_index = inputs
        first_diag = jnp.zeros_like(field_now)
        for step_index in range(FINE):
            extended = jnp.pad(field_now, ((1, 1), (0, 0)))
            divergence, diagonal = flux_terms(extended, padded_rel, padded_sat)
            if step_index == 0:
                first_diag = diagonal
            phase_angle = (slice_index * FINE + step_index).astype(jnp.float32) * scale
            current = source[0] * jnp.cos(phase_angle) + source[1] * jnp.sin(phase_angle)
            field_now = field_now + mobile * (divergence + current)
        return field_now, first_diag

    indices = jnp.arange(SLICES, dtype=jnp.int32)
    cut_slice = (front - 1) % SLICES
    states = start_states
    fine_ends = start_states
    for sweep in range(ITERS):
        fine_ends, diagonals = lax.map(fine_solve, (states, indices))
        decay = 1.0 / (1.0 + FINE * mobile * diagonals)
        decay = jnp.where((indices != cut_slice)[:, None, None], decay, 0.0)
        offset = fine_ends - decay * states

        def compose_step(carry, element):
            joined = compose_maps(carry, element)
            return joined, joined

        unit = (jnp.ones_like(mobile), jnp.zeros_like(mobile))
        final_pair, inclusive = lax.scan(compose_step, unit, (decay, offset))
        incl_decay, incl_offset = inclusive
        closing = incl_offset[-1]
        excl_decay = jnp.concatenate([jnp.ones_like(closing)[None], incl_decay[:-1]], 0)
        excl_offset = jnp.concatenate([jnp.zeros_like(closing)[None], incl_offset[:-1]], 0)
        states = excl_decay * closing + excl_offset
    jumps = jnp.roll(fine_ends, 1, axis=0) - states
    return (states, jumps)
```

```python
import functools
import math

import jax
import jax.numpy as jnp
from jax import lax
from jax.experimental import pallas as pl
from jax.experimental.pallas import tpu as pltpu
from jax.sharding import PartitionSpec as P

FINE = 16
ITERS = 2
GROUP = 4
EARLY = 8
TILE = 8
LANES = 128

RELUCTIVITY = (1.0, 0.3, 1.0, 0.25)
SATURATION = (0.0, 2.0, 0.0, 1.5)
MOBILITY = (0.15, 0.02, 0.0004, 0.0008)

MESH = pl.DeviceIdType.MESH


def lookup(region, table):
    result = jnp.zeros(region.shape, jnp.float32)
    for code, entry in enumerate(table):
        result = jnp.where(region == code, jnp.float32(entry), result)
    return result


def inverse(x):
    guess = pl.reciprocal(x, approx=True)
    return guess * (2.0 - x * guess)


def kernel(
    slices, strips, rows, cols, up_base, total_rows,
    states_in, region_in, source_in, front_ref,
    new_out, jump_out,
    field, region, source, coef_a, coef_b, drive, first,
    decay_own, decay_all, offset_own, offset_all,
    prod_own, prod_all, shift_own, shift_all, solved, end_own, end_prev,
    local_sem, edge_send, edge_recv,
    group_send, group_recv, level_send, level_recv,
    back_send, back_recv, halo_send, halo_recv, end_send, end_recv,
):
    levels = slices // GROUP
    slab = rows // GROUP
    t = lax.axis_index("tm")
    x = lax.axis_index("space")
    level = t // GROUP
    g = t % GROUP
    has_up = x > 0
    has_down = x < strips - 1
    halo = FINE
    groups = total_rows // TILE
    halves = cols // LANES

    def peer(j):
        return level * GROUP + (g + j) % GROUP

    def far(i):
        return ((level + i) % levels) * GROUP + g

    def remote(src, dst, send, recv, tm, space=None):
        return pltpu.make_async_remote_copy(
            src_ref=src, dst_ref=dst, send_sem=send, recv_sem=recv,
            device_id={"tm": tm, "space": x if space is None else space},
            device_id_type=MESH,
        )

    barrier = pltpu.get_barrier_semaphore()

    def greet(tm, space):
        pl.semaphore_signal(
            barrier, inc=1, device_id={"tm": tm, "space": space}, device_id_type=MESH
        )

    expected = (GROUP - 1) + (levels - 1) + 2

    @pl.when(has_up)
    def _():
        for j in range(GROUP):
            greet(peer(j), x - 1)

    @pl.when(has_down)
    def _():
        for j in range(GROUP):
            greet(peer(j), x + 1)

    for j in range(1, GROUP):
        greet(peer(j), x)
    for i in range(1, levels):
        greet(far(i), x)
    greet((t + 1) % slices, x)
    greet((t + slices - 1) % slices, x)

    own = pl.ds(0, rows)
    loads = [
        pltpu.make_async_copy(states_in.at[0], field.at[0, own], local_sem.at[0]),
        pltpu.make_async_copy(region_in, region.at[own], local_sem.at[1]),
        pltpu.make_async_copy(source_in, source.at[:, own], local_sem.at[2]),
    ]
    for copy in loads:
        copy.start()

    cos0, sin0 = jnp.float32(1.0), jnp.float32(0.0)
    for b in range(max(1, (slices - 1).bit_length())):
        on = (t // (1 << b)) % 2 == 1
        angle = 2.0 * math.pi * (1 << b) / slices
        cb = jnp.where(on, jnp.float32(math.cos(angle)), jnp.float32(1.0))
        sb = jnp.where(on, jnp.float32(math.sin(angle)), jnp.float32(0.0))
        cos0, sin0 = cos0 * cb - sin0 * sb, sin0 * cb + cos0 * sb
    cos_d = math.cos(2.0 * math.pi / (slices * FINE))
    sin_d = math.sin(2.0 * math.pi / (slices * FINE))
    cut = lax.rem(front_ref[0] + (slices - 1), slices)
    keep = jnp.where(t == cut, jnp.float32(0.0), jnp.float32(1.0))

    count = expected + GROUP * (has_up.astype(jnp.int32) + has_down.astype(jnp.int32))
    pl.semaphore_wait(barrier, count)

    def edge_copies(way):
        src = pl.ds(0, halo) if way == 0 else pl.ds(rows - halo, halo)
        dst = pl.ds(rows, halo) if way == 0 else pl.ds(up_base, halo)
        to = x - 1 if way == 0 else x + 1
        send, recv = edge_send.at[way], edge_recv.at[way]
        return [
            remote(region_in.at[src], region.at[dst], send.at[0], recv.at[0], t, to),
            remote(states_in.at[0, src], field.at[0, dst], send.at[1], recv.at[1], t, to),
            remote(source_in.at[:, src], source.at[:, dst], send.at[2], recv.at[2], t, to),
        ]

    @pl.when(has_up)
    def _():
        for copy in edge_copies(0):
            copy.start()

    @pl.when(has_down)
    def _():
        for copy in edge_copies(1):
            copy.start()

    for copy in loads:
        copy.wait()

    @pl.when(has_down)
    def _():
        for copy in edge_copies(0):
            copy.wait_recv()

    @pl.when(has_up)
    def _():
        for copy in edge_copies(1):
            copy.wait_recv()

    sub = lax.broadcasted_iota(jnp.int32, (TILE, LANES), 0)
    lane = lax.broadcasted_iota(jnp.int32, (TILE, LANES), 1)
    top, bottom = sub == 0, sub == TILE - 1
    left, right = lane == 0, lane == LANES - 1
    own_groups = rows // TILE

    def neighbours(v):
        down_roll = [[pltpu.roll(a, 1, 0) for a in line] for line in v]
        up_roll = [[pltpu.roll(a, TILE - 1, 0) for a in line] for line in v]
        right_roll = [[pltpu.roll(a, 1, 1) for a in line] for line in v]
        left_roll = [[pltpu.roll(a, LANES - 1, 1) for a in line] for line in v]
        out = []
        for r in range(groups):
            line = []
            for h in range(halves):
                above = down_roll[r - 1][h]
                if r == 0:
                    above = jnp.where(has_up, above, 0.0)
                below = up_roll[(r + 1) % groups][h]
                if r == own_groups - 1:
                    below = jnp.where(has_down, below, 0.0)
                before = right_roll[r][h - 1] if h > 0 else 0.0
                after = left_roll[r][h + 1] if h < halves - 1 else 0.0
                line.append((
                    jnp.where(top, above, down_roll[r][h]),
                    jnp.where(bottom, below, up_roll[r][h]),
                    jnp.where(left, before, right_roll[r][h]),
                    jnp.where(right, after, left_roll[r][h]),
                ))
            out.append(line)
        return out

    def place(r, h):
        return pl.ds(r * TILE, TILE), pl.ds(h * LANES, LANES)

    def tiles(ref, count):
        return [[ref[place(r, h)] for h in range(halves)] for r in range(count)]

    codes = tiles(region, groups)
    relu = [[lookup(c, RELUCTIVITY) for c in line] for line in codes]
    satu = [[lookup(c, SATURATION) for c in line] for line in codes]
    relu_near, satu_near = neighbours(relu), neighbours(satu)
    for r in range(groups):
        for h in range(halves):
            mobile = lookup(codes[r][h], MOBILITY)
            at = place(r, h)
            for f in range(4):
                face_rel = 0.5 * (relu[r][h] + relu_near[r][h][f])
                face_sat = 0.5 * (satu[r][h] + satu_near[r][h][f])
                base = mobile * face_rel
                coef_b[f, *at] = base * face_sat
                coef_a[f, *at] = base + base * face_sat
            drive[0, *at] = mobile * source[0, *at]
            drive[1, *at] = mobile * source[1, *at]

    def step(v, cos_k, sin_k, with_diagonal):
        near = neighbours(v)
        out, diagonals = [], []
        for r in range(groups):
            line, diag_line = [], []
            for h in range(halves):
                at = place(r, h)
                c = v[r][h]
                gain = drive[0, *at] * cos_k + drive[1, *at] * sin_k
                diagonal = None
                for f in range(4):
                    d = near[r][h][f] - c
                    q = coef_a[f, *at] - coef_b[f, *at] * inverse(1.0 + d * d)
                    gain = gain + q * d
                    diagonal = q if diagonal is None else diagonal + q
                line.append(c + gain)
                diag_line.append(diagonal)
            out.append(line)
            diagonals.append(diag_line)
        return (out, diagonals) if with_diagonal else out

    def flat(v):
        return tuple(a for line in v for a in line)

    def nest(v):
        return [list(v[r * halves:(r + 1) * halves]) for r in range(groups)]

    def advance(v, cos_k, sin_k, steps):
        def body(_, carry):
            v, c, s = carry
            v = flat(step(nest(v), c, s, False))
            return v, c * cos_d - s * sin_d, s * cos_d + c * sin_d

        v, cos_k, sin_k = lax.fori_loop(0, steps, body, (flat(v), cos_k, sin_k))
        return nest(v), cos_k, sin_k

    mine = pl.ds(pl.multiple_of(g * slab, slab), slab)

    def group_copies(it, kind, src, dst):
        out = []
        for j in range(1, GROUP):
            to = (g + j) % GROUP
            out.append(remote(
                src.at[it, pl.ds(pl.multiple_of(to * slab, slab), slab)], dst.at[it, g],
                group_send.at[it, kind, j], group_recv.at[it, kind, g], peer(j),
            ))
        return out

    def group_wait(it, kind, dst):
        for j in range(1, GROUP):
            slot = (g + j) % GROUP
            remote(
                dst.at[it, slot], dst.at[it, slot],
                group_send.at[it, kind, j], group_recv.at[it, kind, slot], peer(j),
            ).wait_recv()

    def level_copies(it, kind, src, dst):
        return [
            remote(
                src.at[it], dst.at[it, levels - i - 1],
                level_send.at[it, kind, i], level_recv.at[it, kind, levels - i - 1], far(i),
            )
            for i in range(1, levels)
        ]

    def back_copies(it):
        return [
            remote(
                solved.at[it, (g + j) % GROUP], field.at[it + 1, mine],
                back_send.at[it, j], back_recv.at[it, g], peer(j),
            )
            for j in range(1, GROUP)
        ]

    def back_wait(it):
        for j in range(1, GROUP):
            slot = (g + j) % GROUP
            part = field.at[it + 1, pl.ds(pl.multiple_of(slot * slab, slab), slab)]
            remote(
                part, part, back_send.at[it, j], back_recv.at[it, slot], peer(j)
            ).wait_recv()

    per_halo = halo // slab
    low = g < per_halo
    high = g >= GROUP - per_halo

    def halo_copies(it, way):
        if way == 0:
            start, to = rows + g * slab, x - 1
        else:
            start, to = up_base + (g - (GROUP - per_halo)) * slab, x + 1
        dst = pl.ds(pl.multiple_of(start, slab), slab)
        return [
            remote(
                solved.at[it, (g + j) % GROUP], field.at[it + 1, dst],
                halo_send.at[it, way, j], halo_recv.at[it, way, g], peer(j), to,
            )
            for j in range(GROUP)
        ]

    def halo_wait(it, way):
        for k in range(per_halo):
            slot = k if way == 0 else GROUP - per_halo + k
            start = (rows if way == 0 else up_base) + k * slab
            part = field.at[it + 1, pl.ds(start, slab)]
            remote(
                part, part, halo_send.at[it, way, 0], halo_recv.at[it, way, slot],
                t, x + 1 if way == 0 else x - 1,
            ).wait_recv()

    pending = []
    for it in range(ITERS):
        last = it == ITERS - 1
        start = tiles(field.at[it], groups)
        v, diagonals = step(start, cos0, sin0, True)
        decays = []
        for r in range(own_groups):
            for h in range(halves):
                decay = keep / (1.0 + FINE * diagonals[r][h])
                decay_own[it, *place(r, h)] = decay
        copies = group_copies(it, 0, decay_own, decay_all)
        for copy in copies:
            copy.start()
        pending += copies
        decay_all[it, g] = decay_own[it, mine]

        cos_k, sin_k = cos0 * cos_d - sin0 * sin_d, sin0 * cos_d + cos0 * sin_d
        v, cos_k, sin_k = advance(v, cos_k, sin_k, EARLY)
        group_wait(it, 0, decay_all)
        product = decay_all[it, 0]
        for k in range(1, GROUP):
            product = product * decay_all[it, k]
        prod_own[it] = product
        copies = level_copies(it, 0, prod_own, prod_all)
        for copy in copies:
            copy.start()
        pending += copies
        v, cos_k, sin_k = advance(v, cos_k, sin_k, FINE - 1 - EARLY)

        for r in range(own_groups):
            for h in range(halves):
                at = place(r, h)
                offset_own[it, *at] = v[r][h] - decay_own[it, *at] * field[it, *at]
                if last:
                    end_own[at] = v[r][h]
        copies = group_copies(it, 1, offset_own, offset_all)
        for copy in copies:
            copy.start()
        pending += copies
        if last:
            end_copy = remote(end_own, end_prev, end_send, end_recv, (t + 1) % slices)
            end_copy.start()
            pending.append(end_copy)
        offset_all[it, g] = offset_own[it, mine]
        group_wait(it, 1, offset_all)
        shift = offset_all[it, 0]
        for k in range(1, GROUP):
            shift = decay_all[it, k] * shift + offset_all[it, k]
        shift_own[it] = shift
        copies = level_copies(it, 1, shift_own, shift_all)
        for copy in copies:
            copy.start()
        pending += copies
        for copy in level_copies(it, 0, prod_own, prod_all):
            copy.wait_recv()
        value = shift
        waits = level_copies(it, 1, shift_own, shift_all)
        for r in range(levels - 1):
            waits[levels - 2 - r].wait_recv()
            value = prod_all[it, r] * value + shift_all[it, r]
        solved[it, 0] = value
        for k in range(1, GROUP):
            value = decay_all[it, k - 1] * value + offset_all[it, k - 1]
            solved[it, k] = value
        copies = back_copies(it)
        for copy in copies:
            copy.start()
        pending += copies
        if not last:
            @pl.when(low & has_up)
            def _():
                for copy in halo_copies(it, 0):
                    copy.start()

            @pl.when(high & has_down)
            def _():
                for copy in halo_copies(it, 1):
                    copy.start()

        field[it + 1, mine] = solved[it, g]
        back_wait(it)
        if not last:
            @pl.when(has_down)
            def _():
                halo_wait(it, 0)

            @pl.when(has_up)
            def _():
                halo_wait(it, 1)

    new_out[0] = field[ITERS, own]
    end_copy.wait_recv()
    jump_out[0] = end_prev[...] - field[ITERS, own]

    for copy in pending:
        copy.wait_send()

    @pl.when(has_up)
    def _():
        for copy in edge_copies(0):
            copy.wait_send()

    @pl.when(has_down)
    def _():
        for copy in edge_copies(1):
            copy.wait_send()

    for it in range(ITERS - 1):
        @pl.when(low & has_up)
        def _():
            for copy in halo_copies(it, 0):
                copy.wait_send()

        @pl.when(high & has_down)
        def _():
            for copy in halo_copies(it, 1):
                copy.wait_send()


def solution(mesh):
    slices, strips = mesh.shape["tm"], mesh.shape["space"]

    def on_device(start_states, region_map, source, front):
        _, rows, cols = start_states.shape
        slab = rows // GROUP
        levels = slices // GROUP
        up_base = rows if strips <= 2 else rows + FINE
        total_rows = up_base + FINE
        f32 = jnp.float32
        dma = pltpu.SemaphoreType.DMA
        out = jax.ShapeDtypeStruct((1, rows, cols), f32)
        return pl.pallas_call(
            functools.partial(kernel, slices, strips, rows, cols, up_base, total_rows),
            out_shape=(out, out),
            in_specs=[pl.BlockSpec(memory_space=pl.ANY)] * 3
            + [pl.BlockSpec(memory_space=pltpu.SMEM)],
            out_specs=(pl.BlockSpec(memory_space=pltpu.VMEM),) * 2,
            scratch_shapes=[
                pltpu.VMEM((ITERS + 1, total_rows, cols), f32),
                pltpu.VMEM((total_rows, cols), jnp.int32),
                pltpu.VMEM((2, total_rows, cols), f32),
                pltpu.VMEM((4, total_rows, cols), f32),
                pltpu.VMEM((4, total_rows, cols), f32),
                pltpu.VMEM((2, total_rows, cols), f32),
                pltpu.VMEM((TILE, LANES), f32),
                pltpu.VMEM((ITERS, rows, cols), f32),
                pltpu.VMEM((ITERS, GROUP, slab, cols), f32),
                pltpu.VMEM((ITERS, rows, cols), f32),
                pltpu.VMEM((ITERS, GROUP, slab, cols), f32),
                pltpu.VMEM((ITERS, slab, cols), f32),
                pltpu.VMEM((ITERS, levels - 1, slab, cols), f32),
                pltpu.VMEM((ITERS, slab, cols), f32),
                pltpu.VMEM((ITERS, levels - 1, slab, cols), f32),
                pltpu.VMEM((ITERS, GROUP, slab, cols), f32),
                pltpu.VMEM((rows, cols), f32),
                pltpu.VMEM((rows, cols), f32),
                dma((3,)),
                dma((2, 3)),
                dma((2, 3)),
                dma((ITERS, 2, GROUP)),
                dma((ITERS, 2, GROUP)),
                dma((ITERS, 2, levels)),
                dma((ITERS, 2, levels)),
                dma((ITERS, GROUP)),
                dma((ITERS, GROUP)),
                dma((ITERS, 2, GROUP)),
                dma((ITERS, 2, GROUP)),
                dma,
                dma,
            ],
            compiler_params=pltpu.CompilerParams(
                collective_id=0, has_side_effects=True, vmem_limit_bytes=16 * 2**20
            ),
        )(start_states, region_map, source, jnp.reshape(front, (1,)))

    placed = (P("tm", "space", None), P("space", None), P(None, "space", None), P())
    return jax.shard_map(
        on_device,
        mesh=mesh,
        in_specs=placed,
        out_specs=(P("tm", "space", None), P("tm", "space", None)),
        check_vma=False,
    )
```

```python
import functools
import math

import jax
import jax.numpy as jnp
from jax import lax
from jax.experimental import pallas as pl
from jax.experimental.pallas import tpu as pltpu
from jax.sharding import PartitionSpec as P

FINE = 16
ITERS = 2
GROUP = 4
EARLY = 3
UNROLL = 3
TILE = 8
LANES = 128

RELUCTIVITY = (1.0, 0.3, 1.0, 0.25)
SATURATION = (0.0, 2.0, 0.0, 1.5)
MOBILITY = (0.15, 0.02, 0.0004, 0.0008)

MESH = pl.DeviceIdType.MESH


def lookup(region, table):
    result = jnp.zeros(region.shape, jnp.float32)
    for code, entry in enumerate(table):
        result = jnp.where(region == code, jnp.float32(entry), result)
    return result


def inverse(x):
    guess = pl.reciprocal(x, approx=True)
    return guess * (2.0 - x * guess)


def kernel(
    slices, strips, rows, cols, up_base, total_rows,
    states_in, region_in, source_in, front_ref,
    ends_out,
    field, region, source, coef_a, coef_b, drive,
    decay_own, decay_all, offset_own, offset_all,
    prod_own, prod_all, shift_own, shift_all, solved, end_own, end_prev,
    local_sem, edge_send, edge_recv,
    group_send, group_recv, level_send, level_recv,
    back_send, back_recv, halo_send, halo_recv, end_send, end_recv,
):
    levels = slices // GROUP
    slab = rows // GROUP
    t = lax.axis_index("tm")
    x = lax.axis_index("space")
    level = t // GROUP
    g = t % GROUP
    has_up = x > 0
    has_down = x < strips - 1
    halo = FINE
    groups = total_rows // TILE
    halves = cols // LANES

    def peer(j):
        return level * GROUP + (g + j) % GROUP

    def far(i):
        return ((level + i) % levels) * GROUP + g

    def remote(src, dst, send, recv, tm, space=None):
        return pltpu.make_async_remote_copy(
            src_ref=src, dst_ref=dst, send_sem=send, recv_sem=recv,
            device_id={"tm": tm, "space": x if space is None else space},
            device_id_type=MESH,
        )

    barrier = pltpu.get_barrier_semaphore()

    def greet(tm, space):
        pl.semaphore_signal(
            barrier, inc=1, device_id={"tm": tm, "space": space}, device_id_type=MESH
        )

    expected = (GROUP - 1) + (levels - 1) + 2

    @pl.when(has_up)
    def _():
        for j in range(GROUP):
            greet(peer(j), x - 1)

    @pl.when(has_down)
    def _():
        for j in range(GROUP):
            greet(peer(j), x + 1)

    for j in range(1, GROUP):
        greet(peer(j), x)
    for i in range(1, levels):
        greet(far(i), x)
    greet((t + 1) % slices, x)
    greet((t + slices - 1) % slices, x)

    own = pl.ds(0, rows)
    loads = [
        pltpu.make_async_copy(states_in.at[0], field.at[0, own], local_sem.at[0]),
        pltpu.make_async_copy(region_in, region.at[own], local_sem.at[1]),
        pltpu.make_async_copy(source_in, source.at[:, own], local_sem.at[2]),
    ]
    for copy in loads:
        copy.start()

    cos0, sin0 = jnp.float32(1.0), jnp.float32(0.0)
    for b in range(max(1, (slices - 1).bit_length())):
        on = (t // (1 << b)) % 2 == 1
        angle = 2.0 * math.pi * (1 << b) / slices
        cb = jnp.where(on, jnp.float32(math.cos(angle)), jnp.float32(1.0))
        sb = jnp.where(on, jnp.float32(math.sin(angle)), jnp.float32(0.0))
        cos0, sin0 = cos0 * cb - sin0 * sb, sin0 * cb + cos0 * sb
    cos_d = math.cos(2.0 * math.pi / (slices * FINE))
    sin_d = math.sin(2.0 * math.pi / (slices * FINE))
    cut = lax.rem(front_ref[0] + (slices - 1), slices)
    keep = jnp.where(t == cut, jnp.float32(0.0), jnp.float32(1.0))

    count = expected + GROUP * (has_up.astype(jnp.int32) + has_down.astype(jnp.int32))
    pl.semaphore_wait(barrier, count)

    def edge_copies(way):
        src = pl.ds(0, halo) if way == 0 else pl.ds(rows - halo, halo)
        dst = pl.ds(rows, halo) if way == 0 else pl.ds(up_base, halo)
        to = x - 1 if way == 0 else x + 1
        send, recv = edge_send.at[way], edge_recv.at[way]
        return [
            remote(region_in.at[src], region.at[dst], send.at[0], recv.at[0], t, to),
            remote(states_in.at[0, src], field.at[0, dst], send.at[1], recv.at[1], t, to),
            remote(source_in.at[:, src], source.at[:, dst], send.at[2], recv.at[2], t, to),
        ]

    @pl.when(has_up)
    def _():
        for copy in edge_copies(0):
            copy.start()

    @pl.when(has_down)
    def _():
        for copy in edge_copies(1):
            copy.start()

    for copy in loads:
        copy.wait()

    @pl.when(has_down)
    def _():
        for copy in edge_copies(0):
            copy.wait_recv()

    @pl.when(has_up)
    def _():
        for copy in edge_copies(1):
            copy.wait_recv()

    sub = lax.broadcasted_iota(jnp.int32, (TILE, LANES), 0)
    lane = lax.broadcasted_iota(jnp.int32, (TILE, LANES), 1)
    top, bottom = sub == 0, sub == TILE - 1
    left, right = lane == 0, lane == LANES - 1
    own_groups = rows // TILE

    def neighbours(v):
        down_roll = [[pltpu.roll(a, 1, 0) for a in line] for line in v]
        up_roll = [[pltpu.roll(a, TILE - 1, 0) for a in line] for line in v]
        right_roll = [[pltpu.roll(a, 1, 1) for a in line] for line in v]
        left_roll = [[pltpu.roll(a, LANES - 1, 1) for a in line] for line in v]
        out = []
        for r in range(groups):
            line = []
            for h in range(halves):
                above = down_roll[r - 1][h]
                if r == 0:
                    above = jnp.where(has_up, above, 0.0)
                below = up_roll[(r + 1) % groups][h]
                if r == own_groups - 1:
                    below = jnp.where(has_down, below, 0.0)
                before = right_roll[r][h - 1] if h > 0 else 0.0
                after = left_roll[r][h + 1] if h < halves - 1 else 0.0
                line.append((
                    jnp.where(top, above, down_roll[r][h]),
                    jnp.where(bottom, below, up_roll[r][h]),
                    jnp.where(left, before, right_roll[r][h]),
                    jnp.where(right, after, left_roll[r][h]),
                ))
            out.append(line)
        return out

    def place(r, h):
        return pl.ds(r * TILE, TILE), pl.ds(h * LANES, LANES)

    def tiles(ref, count):
        return [[ref[place(r, h)] for h in range(halves)] for r in range(count)]

    codes = tiles(region, groups)
    relu = [[lookup(c, RELUCTIVITY) for c in line] for line in codes]
    satu = [[lookup(c, SATURATION) for c in line] for line in codes]
    relu_near, satu_near = neighbours(relu), neighbours(satu)
    for r in range(groups):
        for h in range(halves):
            mobile = lookup(codes[r][h], MOBILITY)
            at = place(r, h)
            for f in range(4):
                face_rel = 0.5 * (relu[r][h] + relu_near[r][h][f])
                face_sat = 0.5 * (satu[r][h] + satu_near[r][h][f])
                base = mobile * face_rel
                coef_b[f, *at] = base * face_sat
                coef_a[f, *at] = base + base * face_sat
            drive[0, *at] = mobile * source[0, *at]
            drive[1, *at] = mobile * source[1, *at]

    def step(v, cos_k, sin_k, with_diagonal):
        near = neighbours(v)
        out, diagonals = [], []
        for r in range(groups):
            line, diag_line = [], []
            for h in range(halves):
                at = place(r, h)
                c = v[r][h]
                gain = drive[0, *at] * cos_k + drive[1, *at] * sin_k
                diagonal = None
                for f in range(4):
                    d = near[r][h][f] - c
                    q = coef_a[f, *at] - coef_b[f, *at] * inverse(1.0 + d * d)
                    gain = gain + q * d
                    diagonal = q if diagonal is None else diagonal + q
                line.append(c + gain)
                diag_line.append(diagonal)
            out.append(line)
            diagonals.append(diag_line)
        return (out, diagonals) if with_diagonal else out

    def flat(v):
        return tuple(a for line in v for a in line)

    def nest(v):
        return [list(v[r * halves:(r + 1) * halves]) for r in range(groups)]

    def advance(v, cos_k, sin_k, steps):
        def turn(_, carry):
            v, c, s = carry
            for _ in range(UNROLL):
                v = flat(step(nest(v), c, s, False))
                c, s = c * cos_d - s * sin_d, s * cos_d + c * sin_d
            return v, c, s

        v, cos_k, sin_k = lax.fori_loop(0, steps // UNROLL, turn, (flat(v), cos_k, sin_k))
        return nest(v), cos_k, sin_k

    mine = pl.ds(pl.multiple_of(g * slab, slab), slab)

    def group_copies(it, kind, src, dst):
        out = []
        for j in range(1, GROUP):
            to = (g + j) % GROUP
            out.append(remote(
                src.at[it, pl.ds(pl.multiple_of(to * slab, slab), slab)], dst.at[it, g],
                group_send.at[it, kind, j], group_recv.at[it, kind, g], peer(j),
            ))
        return out

    def group_wait(it, kind, dst):
        for j in range(1, GROUP):
            slot = (g + j) % GROUP
            remote(
                dst.at[it, slot], dst.at[it, slot],
                group_send.at[it, kind, j], group_recv.at[it, kind, slot], peer(j),
            ).wait_recv()

    def level_copies(it, kind, src, dst):
        return [
            remote(
                src.at[it], dst.at[it, levels - i - 1],
                level_send.at[it, kind, i], level_recv.at[it, kind, levels - i - 1], far(i),
            )
            for i in range(1, levels)
        ]

    def back_copies(it):
        return [
            remote(
                solved.at[it, (g + j) % GROUP], field.at[it + 1, mine],
                back_send.at[it, j], back_recv.at[it, g], peer(j),
            )
            for j in range(1, GROUP)
        ]

    def back_wait(it):
        for j in range(1, GROUP):
            slot = (g + j) % GROUP
            part = field.at[it + 1, pl.ds(pl.multiple_of(slot * slab, slab), slab)]
            remote(
                part, part, back_send.at[it, j], back_recv.at[it, slot], peer(j)
            ).wait_recv()

    per_halo = halo // slab
    low = g < per_halo
    high = g >= GROUP - per_halo

    def halo_copies(it, way):
        if way == 0:
            start, to = rows + g * slab, x - 1
        else:
            start, to = up_base + (g - (GROUP - per_halo)) * slab, x + 1
        dst = pl.ds(pl.multiple_of(start, slab), slab)
        return [
            remote(
                solved.at[it, (g + j) % GROUP], field.at[it + 1, dst],
                halo_send.at[it, way, j], halo_recv.at[it, way, g], peer(j), to,
            )
            for j in range(GROUP)
        ]

    def halo_wait(it, way):
        for k in range(per_halo):
            slot = k if way == 0 else GROUP - per_halo + k
            start = (rows if way == 0 else up_base) + k * slab
            part = field.at[it + 1, pl.ds(start, slab)]
            remote(
                part, part, halo_send.at[it, way, 0], halo_recv.at[it, way, slot],
                t, x + 1 if way == 0 else x - 1,
            ).wait_recv()

    pending = []
    for it in range(ITERS):
        last = it == ITERS - 1
        start = tiles(field.at[it], groups)
        v, diagonals = step(start, cos0, sin0, True)
        decays = []
        for r in range(own_groups):
            for h in range(halves):
                decay = keep / (1.0 + FINE * diagonals[r][h])
                decay_own[it, *place(r, h)] = decay
        copies = group_copies(it, 0, decay_own, decay_all)
        for copy in copies:
            copy.start()
        pending += copies
        decay_all[it, g] = decay_own[it, mine]

        cos_k, sin_k = cos0 * cos_d - sin0 * sin_d, sin0 * cos_d + cos0 * sin_d
        v, cos_k, sin_k = advance(v, cos_k, sin_k, EARLY)
        group_wait(it, 0, decay_all)
        product = decay_all[it, 0]
        for k in range(1, GROUP):
            product = product * decay_all[it, k]
        prod_own[it] = product
        copies = level_copies(it, 0, prod_own, prod_all)
        for copy in copies:
            copy.start()
        pending += copies
        v, cos_k, sin_k = advance(v, cos_k, sin_k, FINE - 1 - EARLY)

        for r in range(own_groups):
            for h in range(halves):
                at = place(r, h)
                offset_own[it, *at] = v[r][h] - decay_own[it, *at] * field[it, *at]
                if last:
                    end_own[at] = v[r][h]
        copies = group_copies(it, 1, offset_own, offset_all)
        for copy in copies:
            copy.start()
        pending += copies
        if last:
            end_copy = remote(end_own, end_prev, end_send, end_recv, (t + 1) % slices)
            end_copy.start()
            pending.append(end_copy)
        offset_all[it, g] = offset_own[it, mine]
        group_wait(it, 1, offset_all)
        shift = offset_all[it, 0]
        for k in range(1, GROUP):
            shift = decay_all[it, k] * shift + offset_all[it, k]
        shift_own[it] = shift
        copies = level_copies(it, 1, shift_own, shift_all)
        for copy in copies:
            copy.start()
        pending += copies
        for copy in level_copies(it, 0, prod_own, prod_all):
            copy.wait_recv()
        value = shift
        waits = level_copies(it, 1, shift_own, shift_all)
        for r in range(levels - 1):
            waits[levels - 2 - r].wait_recv()
            value = prod_all[it, r] * value + shift_all[it, r]
        solved[it, 0] = value
        for k in range(1, GROUP):
            value = decay_all[it, k - 1] * value + offset_all[it, k - 1]
            solved[it, k] = value
        copies = back_copies(it)
        for copy in copies:
            copy.start()
        pending += copies
        if not last:
            @pl.when(low & has_up)
            def _():
                for copy in halo_copies(it, 0):
                    copy.start()

            @pl.when(high & has_down)
            def _():
                for copy in halo_copies(it, 1):
                    copy.start()

        field[it + 1, mine] = solved[it, g]
        back_wait(it)
        if not last:
            @pl.when(has_down)
            def _():
                halo_wait(it, 0)

            @pl.when(has_up)
            def _():
                halo_wait(it, 1)

    ends_out[0] = field[ITERS, own]
    end_copy.wait_recv()
    ends_out[1] = end_prev[...]

    for copy in pending:
        copy.wait_send()

    @pl.when(has_up)
    def _():
        for copy in edge_copies(0):
            copy.wait_send()

    @pl.when(has_down)
    def _():
        for copy in edge_copies(1):
            copy.wait_send()

    for it in range(ITERS - 1):
        @pl.when(low & has_up)
        def _():
            for copy in halo_copies(it, 0):
                copy.wait_send()

        @pl.when(high & has_down)
        def _():
            for copy in halo_copies(it, 1):
                copy.wait_send()


def solution(mesh):
    slices, strips = mesh.shape["tm"], mesh.shape["space"]

    def on_device(start_states, region_map, source, front):
        _, rows, cols = start_states.shape
        slab = rows // GROUP
        levels = slices // GROUP
        up_base = rows if strips <= 2 else rows + FINE
        total_rows = up_base + FINE
        f32 = jnp.float32
        dma = pltpu.SemaphoreType.DMA
        ends = pl.pallas_call(
            functools.partial(kernel, slices, strips, rows, cols, up_base, total_rows),
            out_shape=jax.ShapeDtypeStruct((2, rows, cols), f32),
            in_specs=[pl.BlockSpec(memory_space=pltpu.HBM)] * 3
            + [pl.BlockSpec(memory_space=pltpu.SMEM)],
            out_specs=pl.BlockSpec(memory_space=pltpu.VMEM),
            scratch_shapes=[
                pltpu.VMEM((ITERS + 1, total_rows, cols), f32),
                pltpu.VMEM((total_rows, cols), jnp.int32),
                pltpu.VMEM((2, total_rows, cols), f32),
                pltpu.VMEM((4, total_rows, cols), f32),
                pltpu.VMEM((4, total_rows, cols), f32),
                pltpu.VMEM((2, total_rows, cols), f32),
                pltpu.VMEM((ITERS, rows, cols), f32),
                pltpu.VMEM((ITERS, GROUP, slab, cols), f32),
                pltpu.VMEM((ITERS, rows, cols), f32),
                pltpu.VMEM((ITERS, GROUP, slab, cols), f32),
                pltpu.VMEM((ITERS, slab, cols), f32),
                pltpu.VMEM((ITERS, levels - 1, slab, cols), f32),
                pltpu.VMEM((ITERS, slab, cols), f32),
                pltpu.VMEM((ITERS, levels - 1, slab, cols), f32),
                pltpu.VMEM((ITERS, GROUP, slab, cols), f32),
                pltpu.VMEM((rows, cols), f32),
                pltpu.VMEM((rows, cols), f32),
                dma((3,)),
                dma((2, 3)),
                dma((2, 3)),
                dma((ITERS, 2, GROUP)),
                dma((ITERS, 2, GROUP)),
                dma((ITERS, 2, levels)),
                dma((ITERS, 2, levels)),
                dma((ITERS, GROUP)),
                dma((ITERS, GROUP)),
                dma((ITERS, 2, GROUP)),
                dma((ITERS, 2, GROUP)),
                dma,
                dma,
            ],
            compiler_params=pltpu.CompilerParams(
                collective_id=0, has_side_effects=True, vmem_limit_bytes=16 * 2**20
            ),
        )(*(pltpu.with_memory_space_constraint(a, pltpu.HBM) for a in (start_states, region_map, source)), jnp.reshape(front, (1,)))
        return ends[0:1], ends[1:2] - ends[0:1]

    placed = (P("tm", "space", None), P("space", None), P(None, "space", None), P())
    return jax.shard_map(
        on_device,
        mesh=mesh,
        in_specs=placed,
        out_specs=(P("tm", "space", None), P("tm", "space", None)),
        check_vma=False,
    )
```

```python
import functools
import math

import jax
import jax.numpy as jnp
from jax import lax
from jax.experimental import pallas as pl
from jax.experimental.pallas import tpu as pltpu
from jax.sharding import PartitionSpec as P

FINE = 16
ITERS = 2
GROUP = 4
EARLY = 6
TILE = 8
LANES = 128

RELUCTIVITY = (1.0, 0.3, 1.0, 0.25)
SATURATION = (0.0, 2.0, 0.0, 1.5)
MOBILITY = (0.15, 0.02, 0.0004, 0.0008)

MESH = pl.DeviceIdType.MESH


def lookup(region, table):
    result = jnp.zeros(region.shape, jnp.float32)
    for code, entry in enumerate(table):
        result = jnp.where(region == code, jnp.float32(entry), result)
    return result


def inverse(x):
    guess = pl.reciprocal(x, approx=True)
    return guess * (2.0 - x * guess)


def kernel(
    slices, strips, rows, cols, up_base, total_rows,
    states_in, region_in, source_in, front_ref,
    ends_out,
    field, region, source, coef_a, coef_b, drive,
    decay_own, decay_all, offset_own, offset_all,
    prod_own, prod_all, shift_own, shift_all, solved, end_own, end_prev,
    local_sem, edge_send, edge_recv,
    group_send, group_recv, level_send, level_recv,
    back_send, back_recv, halo_send, halo_recv, end_send, end_recv,
):
    levels = slices // GROUP
    slab = rows // GROUP
    t = lax.axis_index("tm")
    x = lax.axis_index("space")
    level = t // GROUP
    g = t % GROUP
    has_up = x > 0
    has_down = x < strips - 1
    halo = FINE
    groups = total_rows // TILE
    halves = cols // LANES

    def peer(j):
        return level * GROUP + (g + j) % GROUP

    def far(i):
        return ((level + i) % levels) * GROUP + g

    def remote(src, dst, send, recv, tm, space=None):
        return pltpu.make_async_remote_copy(
            src_ref=src, dst_ref=dst, send_sem=send, recv_sem=recv,
            device_id={"tm": tm, "space": x if space is None else space},
            device_id_type=MESH,
        )

    barrier = pltpu.get_barrier_semaphore()

    def greet(tm, space):
        pl.semaphore_signal(
            barrier, inc=1, device_id={"tm": tm, "space": space}, device_id_type=MESH
        )

    expected = (GROUP - 1) + (levels - 1) + 2

    @pl.when(has_up)
    def _():
        for j in range(GROUP):
            greet(peer(j), x - 1)

    @pl.when(has_down)
    def _():
        for j in range(GROUP):
            greet(peer(j), x + 1)

    for j in range(1, GROUP):
        greet(peer(j), x)
    for i in range(1, levels):
        greet(far(i), x)
    greet((t + 1) % slices, x)
    greet((t + slices - 1) % slices, x)

    own = pl.ds(0, rows)
    loads = [
        pltpu.make_async_copy(states_in.at[0], field.at[0, own], local_sem.at[0]),
        pltpu.make_async_copy(region_in, region.at[own], local_sem.at[1]),
        pltpu.make_async_copy(source_in, source.at[:, own], local_sem.at[2]),
    ]
    for copy in loads:
        copy.start()

    cos0, sin0 = jnp.float32(1.0), jnp.float32(0.0)
    for b in range(max(1, (slices - 1).bit_length())):
        on = (t // (1 << b)) % 2 == 1
        angle = 2.0 * math.pi * (1 << b) / slices
        cb = jnp.where(on, jnp.float32(math.cos(angle)), jnp.float32(1.0))
        sb = jnp.where(on, jnp.float32(math.sin(angle)), jnp.float32(0.0))
        cos0, sin0 = cos0 * cb - sin0 * sb, sin0 * cb + cos0 * sb
    cos_d = math.cos(2.0 * math.pi / (slices * FINE))
    sin_d = math.sin(2.0 * math.pi / (slices * FINE))
    cut = lax.rem(front_ref[0] + (slices - 1), slices)
    keep = jnp.where(t == cut, jnp.float32(0.0), jnp.float32(1.0))

    count = expected + GROUP * (has_up.astype(jnp.int32) + has_down.astype(jnp.int32))
    for copy in loads:
        copy.wait()
    pl.semaphore_wait(barrier, count)

    def edge_copies(way):
        src = pl.ds(0, halo) if way == 0 else pl.ds(rows - halo, halo)
        dst = pl.ds(rows, halo) if way == 0 else pl.ds(up_base, halo)
        to = x - 1 if way == 0 else x + 1
        send, recv = edge_send.at[way], edge_recv.at[way]
        return [
            remote(region.at[src], region.at[dst], send.at[0], recv.at[0], t, to),
            remote(field.at[0, src], field.at[0, dst], send.at[1], recv.at[1], t, to),
            remote(source.at[:, src], source.at[:, dst], send.at[2], recv.at[2], t, to),
        ]

    @pl.when(has_up)
    def _():
        for copy in edge_copies(0):
            copy.start()

    @pl.when(has_down)
    def _():
        for copy in edge_copies(1):
            copy.start()

    @pl.when(has_down)
    def _():
        for copy in edge_copies(0):
            copy.wait_recv()

    @pl.when(has_up)
    def _():
        for copy in edge_copies(1):
            copy.wait_recv()

    sub = lax.broadcasted_iota(jnp.int32, (TILE, LANES), 0)
    lane = lax.broadcasted_iota(jnp.int32, (TILE, LANES), 1)
    top, bottom = sub == 0, sub == TILE - 1
    left, right = lane == 0, lane == LANES - 1
    own_groups = rows // TILE

    def neighbours(v):
        down_roll = [[pltpu.roll(a, 1, 0) for a in line] for line in v]
        up_roll = [[pltpu.roll(a, TILE - 1, 0) for a in line] for line in v]
        right_roll = [[pltpu.roll(a, 1, 1) for a in line] for line in v]
        left_roll = [[pltpu.roll(a, LANES - 1, 1) for a in line] for line in v]
        out = []
        for r in range(groups):
            line = []
            for h in range(halves):
                above = down_roll[r - 1][h]
                if r == 0:
                    above = jnp.where(has_up, above, 0.0)
                below = up_roll[(r + 1) % groups][h]
                if r == own_groups - 1:
                    below = jnp.where(has_down, below, 0.0)
                before = right_roll[r][h - 1] if h > 0 else 0.0
                after = left_roll[r][h + 1] if h < halves - 1 else 0.0
                line.append((
                    jnp.where(top, above, down_roll[r][h]),
                    jnp.where(bottom, below, up_roll[r][h]),
                    jnp.where(left, before, right_roll[r][h]),
                    jnp.where(right, after, left_roll[r][h]),
                ))
            out.append(line)
        return out

    def place(r, h):
        return pl.ds(r * TILE, TILE), pl.ds(h * LANES, LANES)

    def tiles(ref, count):
        return [[ref[place(r, h)] for h in range(halves)] for r in range(count)]

    codes = tiles(region, groups)
    relu = [[lookup(c, RELUCTIVITY) for c in line] for line in codes]
    satu = [[lookup(c, SATURATION) for c in line] for line in codes]
    relu_near, satu_near = neighbours(relu), neighbours(satu)
    for r in range(groups):
        for h in range(halves):
            mobile = lookup(codes[r][h], MOBILITY)
            at = place(r, h)
            for f in range(4):
                face_rel = 0.5 * (relu[r][h] + relu_near[r][h][f])
                face_sat = 0.5 * (satu[r][h] + satu_near[r][h][f])
                base = mobile * face_rel
                coef_b[f, *at] = base * face_sat
                coef_a[f, *at] = base + base * face_sat
            drive[0, *at] = mobile * source[0, *at]
            drive[1, *at] = mobile * source[1, *at]

    def step(v, cos_k, sin_k):
        near = neighbours(v)
        out, diagonals = [], []
        for r in range(groups):
            line, diag_line = [], []
            for h in range(halves):
                at = place(r, h)
                c = v[r][h]
                gain = drive[0, *at] * cos_k + drive[1, *at] * sin_k
                diagonal = None
                for f in range(4):
                    d = near[r][h][f] - c
                    q = coef_a[f, *at] - coef_b[f, *at] * inverse(1.0 + d * d)
                    gain = gain + q * d
                    diagonal = q if diagonal is None else diagonal + q
                line.append(c + gain)
                diag_line.append(diagonal)
            out.append(line)
            diagonals.append(diag_line)
        return out, diagonals

    def flat(v):
        return tuple(a for line in v for a in line)

    def nest(v):
        return [list(v[r * halves:(r + 1) * halves]) for r in range(groups)]

    mine = pl.ds(pl.multiple_of(g * slab, slab), slab)

    def group_copies(it, kind, src, dst):
        out = []
        for j in range(1, GROUP):
            to = (g + j) % GROUP
            out.append(remote(
                src.at[it, pl.ds(pl.multiple_of(to * slab, slab), slab)], dst.at[it, g],
                group_send.at[it, kind, j], group_recv.at[it, kind, g], peer(j),
            ))
        return out

    def group_wait(it, kind, dst):
        for j in range(1, GROUP):
            slot = (g + j) % GROUP
            remote(
                dst.at[it, slot], dst.at[it, slot],
                group_send.at[it, kind, j], group_recv.at[it, kind, slot], peer(j),
            ).wait_recv()

    def level_copies(it, kind, src, dst):
        return [
            remote(
                src.at[it], dst.at[it, levels - i - 1],
                level_send.at[it, kind, i], level_recv.at[it, kind, levels - i - 1], far(i),
            )
            for i in range(1, levels)
        ]

    def back_copies(it):
        return [
            remote(
                solved.at[it, (g + j) % GROUP], field.at[it + 1, mine],
                back_send.at[it, j], back_recv.at[it, g], peer(j),
            )
            for j in range(1, GROUP)
        ]

    def back_wait(it):
        for j in range(1, GROUP):
            slot = (g + j) % GROUP
            part = field.at[it + 1, pl.ds(pl.multiple_of(slot * slab, slab), slab)]
            remote(
                part, part, back_send.at[it, j], back_recv.at[it, slot], peer(j)
            ).wait_recv()

    per_halo = halo // slab
    low = g < per_halo
    high = g >= GROUP - per_halo

    def halo_copies(it, way):
        if way == 0:
            start, to = rows + g * slab, x - 1
        else:
            start, to = up_base + (g - (GROUP - per_halo)) * slab, x + 1
        dst = pl.ds(pl.multiple_of(start, slab), slab)
        return [
            remote(
                solved.at[it, (g + j) % GROUP], field.at[it + 1, dst],
                halo_send.at[it, way, j], halo_recv.at[it, way, g], peer(j), to,
            )
            for j in range(GROUP)
        ]

    def halo_wait(it, way):
        for k in range(per_halo):
            slot = k if way == 0 else GROUP - per_halo + k
            start = (rows if way == 0 else up_base) + k * slab
            part = field.at[it + 1, pl.ds(start, slab)]
            remote(
                part, part, halo_send.at[it, way, 0], halo_recv.at[it, way, slot],
                t, x + 1 if way == 0 else x - 1,
            ).wait_recv()

    def start_all(copies):
        for copy in copies:
            copy.start()

    def sent_all(copies):
        for copy in copies:
            copy.wait_send()

    def end_copy():
        return remote(end_own, end_prev, end_send, end_recv, (t + 1) % slices)

    def sweep(it, _):
        more = it < ITERS - 1

        def turn(k, carry):
            v, cos_k, sin_k = carry
            v, diagonals = step(nest(v), cos_k, sin_k)

            @pl.when(k == 0)
            def _():
                for r in range(own_groups):
                    for h in range(halves):
                        decay_own[it, *place(r, h)] = keep / (1.0 + FINE * diagonals[r][h])
                start_all(group_copies(it, 0, decay_own, decay_all))
                decay_all[it, g] = decay_own[it, mine]

            @pl.when(k == EARLY)
            def _():
                group_wait(it, 0, decay_all)
                product = decay_all[it, 0]
                for j in range(1, GROUP):
                    product = product * decay_all[it, j]
                prod_own[it] = product
                start_all(level_copies(it, 0, prod_own, prod_all))

            return flat(v), cos_k * cos_d - sin_k * sin_d, sin_k * cos_d + cos_k * sin_d

        begin = flat(tiles(field.at[it], groups))
        v, _, _ = lax.fori_loop(0, FINE, turn, (begin, cos0, sin0))
        v = nest(v)
        for r in range(own_groups):
            for h in range(halves):
                at = place(r, h)
                offset_own[it, *at] = v[r][h] - decay_own[it, *at] * field[it, *at]
                end_own[at] = v[r][h]
        start_all(group_copies(it, 1, offset_own, offset_all))
        offset_all[it, g] = offset_own[it, mine]

        @pl.when(jnp.logical_not(more))
        def _():
            end_copy().start()

        group_wait(it, 1, offset_all)
        shift = offset_all[it, 0]
        for k in range(1, GROUP):
            shift = decay_all[it, k] * shift + offset_all[it, k]
        shift_own[it] = shift
        start_all(level_copies(it, 1, shift_own, shift_all))
        for copy in level_copies(it, 0, prod_own, prod_all):
            copy.wait_recv()
        value = shift
        waits = level_copies(it, 1, shift_own, shift_all)
        for r in range(levels - 1):
            waits[levels - 2 - r].wait_recv()
            value = prod_all[it, r] * value + shift_all[it, r]
        solved[it, 0] = value
        for k in range(1, GROUP):
            value = decay_all[it, k - 1] * value + offset_all[it, k - 1]
            solved[it, k] = value
        start_all(back_copies(it))

        @pl.when(more & low & has_up)
        def _():
            start_all(halo_copies(it, 0))

        @pl.when(more & high & has_down)
        def _():
            start_all(halo_copies(it, 1))

        field[it + 1, mine] = solved[it, g]
        back_wait(it)

        @pl.when(more & has_down)
        def _():
            halo_wait(it, 0)

        @pl.when(more & has_up)
        def _():
            halo_wait(it, 1)

        sent_all(group_copies(it, 0, decay_own, decay_all))
        sent_all(group_copies(it, 1, offset_own, offset_all))
        sent_all(level_copies(it, 0, prod_own, prod_all))
        sent_all(level_copies(it, 1, shift_own, shift_all))
        sent_all(back_copies(it))

        @pl.when(more & low & has_up)
        def _():
            sent_all(halo_copies(it, 0))

        @pl.when(more & high & has_down)
        def _():
            sent_all(halo_copies(it, 1))

        return 0

    lax.fori_loop(0, ITERS, sweep, 0)

    ends_out[0] = field[ITERS, own]
    end_copy().wait_recv()
    ends_out[1] = end_prev[...]
    end_copy().wait_send()

    @pl.when(has_up)
    def _():
        sent_all(edge_copies(0))

    @pl.when(has_down)
    def _():
        sent_all(edge_copies(1))


def solution(mesh):
    slices, strips = mesh.shape["tm"], mesh.shape["space"]

    def on_device(start_states, region_map, source, front):
        _, rows, cols = start_states.shape
        slab = rows // GROUP
        levels = slices // GROUP
        up_base = rows if strips <= 2 else rows + FINE
        total_rows = up_base + FINE
        f32 = jnp.float32
        dma = pltpu.SemaphoreType.DMA
        ends = pl.pallas_call(
            functools.partial(kernel, slices, strips, rows, cols, up_base, total_rows),
            out_shape=jax.ShapeDtypeStruct((2, rows, cols), f32),
            in_specs=[pl.BlockSpec(memory_space=pltpu.HBM)] * 3
            + [pl.BlockSpec(memory_space=pltpu.SMEM)],
            out_specs=pl.BlockSpec(memory_space=pltpu.VMEM),
            scratch_shapes=[
                pltpu.VMEM((ITERS + 1, total_rows, cols), f32),
                pltpu.VMEM((total_rows, cols), jnp.int32),
                pltpu.VMEM((2, total_rows, cols), f32),
                pltpu.VMEM((4, total_rows, cols), f32),
                pltpu.VMEM((4, total_rows, cols), f32),
                pltpu.VMEM((2, total_rows, cols), f32),
                pltpu.VMEM((ITERS, rows, cols), f32),
                pltpu.VMEM((ITERS, GROUP, slab, cols), f32),
                pltpu.VMEM((ITERS, rows, cols), f32),
                pltpu.VMEM((ITERS, GROUP, slab, cols), f32),
                pltpu.VMEM((ITERS, slab, cols), f32),
                pltpu.VMEM((ITERS, levels - 1, slab, cols), f32),
                pltpu.VMEM((ITERS, slab, cols), f32),
                pltpu.VMEM((ITERS, levels - 1, slab, cols), f32),
                pltpu.VMEM((ITERS, GROUP, slab, cols), f32),
                pltpu.VMEM((rows, cols), f32),
                pltpu.VMEM((rows, cols), f32),
                dma((3,)),
                dma((2, 3)),
                dma((2, 3)),
                dma((ITERS, 2, GROUP)),
                dma((ITERS, 2, GROUP)),
                dma((ITERS, 2, levels)),
                dma((ITERS, 2, levels)),
                dma((ITERS, GROUP)),
                dma((ITERS, GROUP)),
                dma((ITERS, 2, GROUP)),
                dma((ITERS, 2, GROUP)),
                dma,
                dma,
            ],
            compiler_params=pltpu.CompilerParams(
                collective_id=0, has_side_effects=True, vmem_limit_bytes=16 * 2**20
            ),
        )(*(pltpu.with_memory_space_constraint(a, pltpu.HBM) for a in (start_states, region_map, source)), jnp.reshape(front, (1,)))
        return ends[0:1], ends[1:2] - ends[0:1]

    placed = (P("tm", "space", None), P("space", None), P(None, "space", None), P())
    return jax.shard_map(
        on_device,
        mesh=mesh,
        in_specs=placed,
        out_specs=(P("tm", "space", None), P("tm", "space", None)),
        check_vma=False,
    )
```

```python
import functools
import math

import jax
import jax.numpy as jnp
from jax import lax
from jax.experimental import pallas as pl
from jax.experimental.pallas import tpu as pltpu
from jax.sharding import PartitionSpec as P

FINE = 16
ITERS = 2
GROUP = 4
DECAY_AT = 5
PRODUCT_AT = 11
TILE = 8
LANES = 128

RELUCTIVITY = (1.0, 0.3, 1.0, 0.25)
SATURATION = (0.0, 2.0, 0.0, 1.5)
MOBILITY = (0.15, 0.02, 0.0004, 0.0008)

MESH = pl.DeviceIdType.MESH


def lookup(region, table):
    result = jnp.zeros(region.shape, jnp.float32)
    for code, entry in enumerate(table):
        result = jnp.where(region == code, jnp.float32(entry), result)
    return result


def inverse(x):
    guess = pl.reciprocal(x, approx=True)
    return guess * (2.0 - x * guess)


def grid(slices):
    t = lax.axis_index("tm")
    return t, lax.axis_index("space"), t // GROUP, t % GROUP, slices // GROUP


def send_to(src, dst, send, recv, tm, space):
    return pltpu.make_async_remote_copy(
        src_ref=src, dst_ref=dst, send_sem=send, recv_sem=recv,
        device_id={"tm": tm, "space": space}, device_id_type=MESH,
    )


def edge_kernel(
    strips, rows, up_base,
    states_in, region_in, source_in,
    field_out, region_out, source_out,
    field, region, source, local_sem, edge_send, edge_recv,
):
    t, x = lax.axis_index("tm"), lax.axis_index("space")
    has_up = x > 0
    has_down = x < strips - 1
    halo = FINE
    barrier = pltpu.get_barrier_semaphore()

    def greet(space):
        pl.semaphore_signal(
            barrier, inc=1, device_id={"tm": t, "space": space}, device_id_type=MESH
        )

    @pl.when(has_up)
    def _():
        greet(x - 1)

    @pl.when(has_down)
    def _():
        greet(x + 1)

    own = pl.ds(0, rows)
    loads = [
        pltpu.make_async_copy(states_in.at[0], field.at[own], local_sem.at[0]),
        pltpu.make_async_copy(region_in, region.at[own], local_sem.at[1]),
        pltpu.make_async_copy(source_in, source.at[:, own], local_sem.at[2]),
    ]
    for copy in loads:
        copy.start()
    for copy in loads:
        copy.wait()
    pl.semaphore_wait(barrier, has_up.astype(jnp.int32) + has_down.astype(jnp.int32))

    def edge_copies(way):
        src = pl.ds(0, halo) if way == 0 else pl.ds(rows - halo, halo)
        dst = pl.ds(rows, halo) if way == 0 else pl.ds(up_base, halo)
        to = x - 1 if way == 0 else x + 1
        send, recv = edge_send.at[way], edge_recv.at[way]
        return [
            send_to(source.at[:, src], source.at[:, dst], send.at[2], recv.at[2], t, to),
            send_to(region.at[src], region.at[dst], send.at[0], recv.at[0], t, to),
            send_to(field.at[src], field.at[dst], send.at[1], recv.at[1], t, to),
        ]

    @pl.when(has_up)
    def _():
        for copy in edge_copies(0):
            copy.start()

    @pl.when(has_down)
    def _():
        for copy in edge_copies(1):
            copy.start()

    field_out[own] = field[own]
    region_out[own] = region[own]
    source_out[:, own] = source[:, own]

    @pl.when(has_down)
    def _():
        for copy in edge_copies(0):
            copy.wait_recv()
        at = pl.ds(rows, halo)
        field_out[at] = field[at]
        region_out[at] = region[at]
        source_out[:, at] = source[:, at]

    @pl.when(has_up)
    def _():
        for copy in edge_copies(1):
            copy.wait_recv()
        at = pl.ds(up_base, halo)
        field_out[at] = field[at]
        region_out[at] = region[at]
        source_out[:, at] = source[:, at]

    @pl.when(has_up)
    def _():
        for copy in edge_copies(0):
            copy.wait_send()

    @pl.when(has_down)
    def _():
        for copy in edge_copies(1):
            copy.wait_send()


def kernel(
    slices, strips, rows, cols, up_base, total_rows,
    begin, region, source, front_ref,
    ends_out,
    field, coef_a, coef_b, drive,
    decay_own, decay_all, offset_own, offset_all,
    prod_own, prod_all, shift_own, shift_all, solved, end_own, end_prev,
    group_send, group_recv, level_send, level_recv,
    back_send, back_recv, halo_send, halo_recv, end_send, end_recv,
):
    t, x, level, g, levels = grid(slices)
    slab = rows // GROUP
    has_up = x > 0
    has_down = x < strips - 1
    halo = FINE
    groups = total_rows // TILE
    halves = cols // LANES

    def peer(j):
        return level * GROUP + (g + j) % GROUP

    def far(i):
        return ((level + i) % levels) * GROUP + g

    def remote(src, dst, send, recv, tm, space=None):
        return send_to(src, dst, send, recv, tm, x if space is None else space)

    barrier = pltpu.get_barrier_semaphore()

    def greet(tm, space):
        pl.semaphore_signal(
            barrier, inc=1, device_id={"tm": tm, "space": space}, device_id_type=MESH
        )

    expected = (GROUP - 1) + (levels - 1) + 2

    @pl.when(has_up)
    def _():
        for j in range(GROUP):
            greet(peer(j), x - 1)

    @pl.when(has_down)
    def _():
        for j in range(GROUP):
            greet(peer(j), x + 1)

    for j in range(1, GROUP):
        greet(peer(j), x)
    for i in range(1, levels):
        greet(far(i), x)
    greet((t + 1) % slices, x)
    greet((t + slices - 1) % slices, x)

    own = pl.ds(0, rows)
    cos0, sin0 = jnp.float32(1.0), jnp.float32(0.0)
    for b in range(max(1, (slices - 1).bit_length())):
        on = (t // (1 << b)) % 2 == 1
        angle = 2.0 * math.pi * (1 << b) / slices
        cb = jnp.where(on, jnp.float32(math.cos(angle)), jnp.float32(1.0))
        sb = jnp.where(on, jnp.float32(math.sin(angle)), jnp.float32(0.0))
        cos0, sin0 = cos0 * cb - sin0 * sb, sin0 * cb + cos0 * sb
    cos_d = math.cos(2.0 * math.pi / (slices * FINE))
    sin_d = math.sin(2.0 * math.pi / (slices * FINE))
    cut = lax.rem(front_ref[0] + (slices - 1), slices)
    keep = jnp.where(t == cut, jnp.float32(0.0), jnp.float32(1.0))

    count = expected + GROUP * (has_up.astype(jnp.int32) + has_down.astype(jnp.int32))
    sub = lax.broadcasted_iota(jnp.int32, (TILE, LANES), 0)
    lane = lax.broadcasted_iota(jnp.int32, (TILE, LANES), 1)
    top, bottom = sub == 0, sub == TILE - 1
    left, right = lane == 0, lane == LANES - 1
    own_groups = rows // TILE

    def neighbours(v):
        down_roll = [[pltpu.roll(a, 1, 0) for a in line] for line in v]
        up_roll = [[pltpu.roll(a, TILE - 1, 0) for a in line] for line in v]
        right_roll = [[pltpu.roll(a, 1, 1) for a in line] for line in v]
        left_roll = [[pltpu.roll(a, LANES - 1, 1) for a in line] for line in v]
        out = []
        for r in range(groups):
            line = []
            for h in range(halves):
                above = down_roll[r - 1][h]
                if r == 0:
                    above = jnp.where(has_up, above, 0.0)
                below = up_roll[(r + 1) % groups][h]
                if r == own_groups - 1:
                    below = jnp.where(has_down, below, 0.0)
                before = right_roll[r][h - 1] if h > 0 else 0.0
                after = left_roll[r][h + 1] if h < halves - 1 else 0.0
                line.append((
                    jnp.where(top, above, down_roll[r][h]),
                    jnp.where(bottom, below, up_roll[r][h]),
                    jnp.where(left, before, right_roll[r][h]),
                    jnp.where(right, after, left_roll[r][h]),
                ))
            out.append(line)
        return out

    def place(r, h):
        return pl.ds(r * TILE, TILE), pl.ds(h * LANES, LANES)

    def tiles(ref, count):
        return [[ref[place(r, h)] for h in range(halves)] for r in range(count)]

    codes = tiles(region, groups)
    relu = [[lookup(c, RELUCTIVITY) for c in line] for line in codes]
    satu = [[lookup(c, SATURATION) for c in line] for line in codes]
    relu_near, satu_near = neighbours(relu), neighbours(satu)
    for r in range(groups):
        for h in range(halves):
            mobile = lookup(codes[r][h], MOBILITY)
            at = place(r, h)
            for f in range(4):
                face_rel = 0.5 * (relu[r][h] + relu_near[r][h][f])
                face_sat = 0.5 * (satu[r][h] + satu_near[r][h][f])
                base = mobile * face_rel
                coef_b[f, *at] = base * face_sat
                coef_a[f, *at] = base + base * face_sat
            drive[0, *at] = mobile * source[0, *at]
            drive[1, *at] = mobile * source[1, *at]

    def step(v, cos_k, sin_k):
        near = neighbours(v)
        out, diagonals = [], []
        for r in range(groups):
            line, diag_line = [], []
            for h in range(halves):
                at = place(r, h)
                c = v[r][h]
                gain = drive[0, *at] * cos_k + drive[1, *at] * sin_k
                diagonal = None
                for f in range(4):
                    d = near[r][h][f] - c
                    q = coef_a[f, *at] - coef_b[f, *at] * inverse(1.0 + d * d)
                    gain = gain + q * d
                    diagonal = q if diagonal is None else diagonal + q
                line.append(c + gain)
                diag_line.append(diagonal)
            out.append(line)
            diagonals.append(diag_line)
        return out, diagonals

    def flat(v):
        return tuple(a for line in v for a in line)

    def nest(v):
        return [list(v[r * halves:(r + 1) * halves]) for r in range(groups)]

    mine = pl.ds(pl.multiple_of(g * slab, slab), slab)

    def group_copies(it, kind, src, dst):
        out = []
        for j in range(1, GROUP):
            to = (g + j) % GROUP
            out.append(remote(
                src.at[it, pl.ds(pl.multiple_of(to * slab, slab), slab)], dst.at[it, g],
                group_send.at[it, kind, j], group_recv.at[it, kind, g], peer(j),
            ))
        return out

    def group_wait(it, kind, dst):
        for j in range(1, GROUP):
            slot = (g + j) % GROUP
            remote(
                dst.at[it, slot], dst.at[it, slot],
                group_send.at[it, kind, j], group_recv.at[it, kind, slot], peer(j),
            ).wait_recv()

    def level_copies(it, kind, src, dst):
        return [
            remote(
                src.at[it], dst.at[it, levels - i - 1],
                level_send.at[it, kind, i], level_recv.at[it, kind, levels - i - 1], far(i),
            )
            for i in (*range(levels - 1, 0, -1),)
        ]

    def back_copies(it):
        return [
            remote(
                solved.at[it, (g + j) % GROUP], field.at[it + 1, mine],
                back_send.at[it, j], back_recv.at[it, g], peer(j),
            )
            for j in range(1, GROUP)
        ]

    def back_wait(it):
        for j in range(1, GROUP):
            slot = (g + j) % GROUP
            part = field.at[it + 1, pl.ds(pl.multiple_of(slot * slab, slab), slab)]
            remote(
                part, part, back_send.at[it, j], back_recv.at[it, slot], peer(j)
            ).wait_recv()

    per_halo = halo // slab
    low = g < per_halo
    high = g >= GROUP - per_halo

    def halo_copies(it, way):
        if way == 0:
            start, to = rows + g * slab, x - 1
        else:
            start, to = up_base + (g - (GROUP - per_halo)) * slab, x + 1
        dst = pl.ds(pl.multiple_of(start, slab), slab)
        return [
            remote(
                solved.at[it, (g + j) % GROUP], field.at[it + 1, dst],
                halo_send.at[it, way, j], halo_recv.at[it, way, g], peer(j), to,
            )
            for j in range(GROUP)
        ]

    def halo_wait(it, way):
        for k in range(per_halo):
            slot = k if way == 0 else GROUP - per_halo + k
            start = (rows if way == 0 else up_base) + k * slab
            part = field.at[it + 1, pl.ds(start, slab)]
            remote(
                part, part, halo_send.at[it, way, 0], halo_recv.at[it, way, slot],
                t, x + 1 if way == 0 else x - 1,
            ).wait_recv()

    def start_all(copies):
        for copy in copies:
            copy.start()

    def sent_all(copies):
        for copy in copies:
            copy.wait_send()

    def end_copy():
        return remote(end_own, end_prev, end_send, end_recv, (t + 1) % slices)

    for r in range(groups):
        for h in range(halves):
            field[0, *place(r, h)] = begin[place(r, h)]

    def sweep(it, _):
        more = it < ITERS - 1

        def turn(k, carry):
            v, cos_k, sin_k = carry
            v, diagonals = step(nest(v), cos_k, sin_k)

            @pl.when(k == 0)
            def _():
                for r in range(own_groups):
                    for h in range(halves):
                        decay_own[it, *place(r, h)] = keep / (1.0 + FINE * diagonals[r][h])

            @pl.when((it == 0) & (k == DECAY_AT))
            def _():
                pl.semaphore_wait(barrier, count)

            @pl.when(k == DECAY_AT)
            def _():
                start_all(group_copies(it, 0, decay_own, decay_all))
                decay_all[it, g] = decay_own[it, mine]

            @pl.when(k == PRODUCT_AT)
            def _():
                group_wait(it, 0, decay_all)
                product = decay_all[it, 0]
                for j in range(1, GROUP):
                    product = product * decay_all[it, j]
                prod_own[it] = product
                start_all(level_copies(it, 0, prod_own, prod_all))

            return flat(v), cos_k * cos_d - sin_k * sin_d, sin_k * cos_d + cos_k * sin_d

        v, _, _ = lax.fori_loop(0, FINE, turn, (flat(tiles(field.at[it], groups)), cos0, sin0))
        v = nest(v)
        for r in range(own_groups):
            for h in range(halves):
                at = place(r, h)
                offset_own[it, *at] = v[r][h] - decay_own[it, *at] * field[it, *at]
                end_own[at] = v[r][h]
        start_all(group_copies(it, 1, offset_own, offset_all))
        offset_all[it, g] = offset_own[it, mine]

        @pl.when(jnp.logical_not(more))
        def _():
            end_copy().start()

        group_wait(it, 1, offset_all)
        shift = offset_all[it, 0]
        for k in range(1, GROUP):
            shift = decay_all[it, k] * shift + offset_all[it, k]
        shift_own[it] = shift
        start_all(level_copies(it, 1, shift_own, shift_all))
        for copy in level_copies(it, 0, prod_own, prod_all):
            copy.wait_recv()
        value = shift
        waits = level_copies(it, 1, shift_own, shift_all)
        for r in range(levels - 1):
            waits[r].wait_recv()
            value = prod_all[it, r] * value + shift_all[it, r]
        solved[it, 0] = value
        for k in range(1, GROUP):
            value = decay_all[it, k - 1] * value + offset_all[it, k - 1]
            solved[it, k] = value
        start_all(back_copies(it))

        @pl.when(more & low & has_up)
        def _():
            start_all(halo_copies(it, 0))

        @pl.when(more & high & has_down)
        def _():
            start_all(halo_copies(it, 1))

        field[it + 1, mine] = solved[it, g]
        back_wait(it)

        @pl.when(more & has_down)
        def _():
            halo_wait(it, 0)

        @pl.when(more & has_up)
        def _():
            halo_wait(it, 1)

        sent_all(group_copies(it, 0, decay_own, decay_all))
        sent_all(group_copies(it, 1, offset_own, offset_all))
        sent_all(level_copies(it, 0, prod_own, prod_all))
        sent_all(level_copies(it, 1, shift_own, shift_all))
        sent_all(back_copies(it))

        @pl.when(more & low & has_up)
        def _():
            sent_all(halo_copies(it, 0))

        @pl.when(more & high & has_down)
        def _():
            sent_all(halo_copies(it, 1))

        return 0

    lax.fori_loop(0, ITERS, sweep, 0)

    ends_out[0] = field[ITERS, own]
    end_copy().wait_recv()
    ends_out[1] = end_prev[...]
    end_copy().wait_send()


def solution(mesh):
    slices, strips = mesh.shape["tm"], mesh.shape["space"]

    def on_device(start_states, region_map, source, front):
        _, rows, cols = start_states.shape
        slab = rows // GROUP
        levels = slices // GROUP
        up_base = rows if strips <= 2 else rows + FINE
        total_rows = up_base + FINE
        f32 = jnp.float32
        dma = pltpu.SemaphoreType.DMA
        vmem = pl.BlockSpec(memory_space=pltpu.VMEM)
        shapes = [
            ((total_rows, cols), f32),
            ((total_rows, cols), jnp.int32),
            ((2, total_rows, cols), f32),
        ]
        wide = pl.pallas_call(
            functools.partial(edge_kernel, strips, rows, up_base),
            out_shape=[jax.ShapeDtypeStruct(*shape) for shape in shapes],
            in_specs=[pl.BlockSpec(memory_space=pltpu.HBM)] * 3,
            out_specs=[vmem] * 3,
            scratch_shapes=[pltpu.VMEM(*shape) for shape in shapes]
            + [dma((3,)), dma((2, 3)), dma((2, 3))],
            compiler_params=pltpu.CompilerParams(
                collective_id=0, has_side_effects=True, vmem_limit_bytes=16 * 2**20
            ),
        )(*(
            pltpu.with_memory_space_constraint(a, pltpu.HBM)
            for a in (start_states, region_map, source)
        ))
        ends = pl.pallas_call(
            functools.partial(kernel, slices, strips, rows, cols, up_base, total_rows),
            out_shape=jax.ShapeDtypeStruct((2, rows, cols), f32),
            in_specs=[vmem] * 3 + [pl.BlockSpec(memory_space=pltpu.SMEM)],
            out_specs=vmem,
            scratch_shapes=[
                pltpu.VMEM((ITERS + 1, total_rows, cols), f32),
                pltpu.VMEM((4, total_rows, cols), f32),
                pltpu.VMEM((4, total_rows, cols), f32),
                pltpu.VMEM((2, total_rows, cols), f32),
                pltpu.VMEM((ITERS, rows, cols), f32),
                pltpu.VMEM((ITERS, GROUP, slab, cols), f32),
                pltpu.VMEM((ITERS, rows, cols), f32),
                pltpu.VMEM((ITERS, GROUP, slab, cols), f32),
                pltpu.VMEM((ITERS, slab, cols), f32),
                pltpu.VMEM((ITERS, levels - 1, slab, cols), f32),
                pltpu.VMEM((ITERS, slab, cols), f32),
                pltpu.VMEM((ITERS, levels - 1, slab, cols), f32),
                pltpu.VMEM((ITERS, GROUP, slab, cols), f32),
                pltpu.VMEM((rows, cols), f32),
                pltpu.VMEM((rows, cols), f32),
                dma((ITERS, 2, GROUP)),
                dma((ITERS, 2, GROUP)),
                dma((ITERS, 2, levels)),
                dma((ITERS, 2, levels)),
                dma((ITERS, GROUP)),
                dma((ITERS, GROUP)),
                dma((ITERS, 2, GROUP)),
                dma((ITERS, 2, GROUP)),
                dma,
                dma,
            ],
            compiler_params=pltpu.CompilerParams(
                collective_id=1, has_side_effects=True, vmem_limit_bytes=16 * 2**20
            ),
        )(*wide, jnp.reshape(front, (1,)))
        return ends[0:1], ends[1:2] - ends[0:1]

    placed = (P("tm", "space", None), P("space", None), P(None, "space", None), P())
    return jax.shard_map(
        on_device,
        mesh=mesh,
        in_specs=placed,
        out_specs=(P("tm", "space", None), P("tm", "space", None)),
        check_vma=False,
    )
```

```python
import functools
import math

import jax
import jax.numpy as jnp
from jax import lax
from jax.experimental import pallas as pl
from jax.experimental.pallas import tpu as pltpu
from jax.sharding import PartitionSpec as P

FINE = 16
ITERS = 2
GROUP = 4
DECAY_AT = 5
PRODUCT_AT = 11
TILE = 8
LANES = 128

RELUCTIVITY = (1.0, 0.3, 1.0, 0.25)
SATURATION = (0.0, 2.0, 0.0, 1.5)
MOBILITY = (0.15, 0.02, 0.0004, 0.0008)

MESH = pl.DeviceIdType.MESH


def lookup(region, table):
    result = jnp.zeros(region.shape, jnp.float32)
    for code, entry in enumerate(table):
        result = jnp.where(region == code, jnp.float32(entry), result)
    return result


def weight(d, a, b):
    return a - b * pl.reciprocal(1.0 + d * d, approx=True)


def columns_apart(rows_to):
    i = lax.broadcasted_iota(jnp.int32, (2 * LANES, 2 * LANES), 0)
    j = lax.broadcasted_iota(jnp.int32, (2 * LANES, 2 * LANES), 1)
    column, spot = (i, j) if rows_to else (j, i)
    return (column == 2 * (spot % LANES) + spot // LANES).astype(jnp.float32)


def moved(block, order):
    return jnp.dot(
        block, order, precision=lax.Precision.HIGHEST, preferred_element_type=jnp.float32
    )


def grid(slices):
    t = lax.axis_index("tm")
    return t, lax.axis_index("space"), t // GROUP, t % GROUP, slices // GROUP


def send_to(src, dst, send, recv, tm, space):
    return pltpu.make_async_remote_copy(
        src_ref=src, dst_ref=dst, send_sem=send, recv_sem=recv,
        device_id={"tm": tm, "space": space}, device_id_type=MESH,
    )


def edge_kernel(
    strips, rows, up_base,
    states_in, region_in, source_in,
    field_out, region_out, source_out,
    field, region, source, local_sem, edge_send, edge_recv,
):
    t, x = lax.axis_index("tm"), lax.axis_index("space")
    has_up = x > 0
    has_down = x < strips - 1
    halo = FINE
    barrier = pltpu.get_barrier_semaphore()

    def greet(space):
        pl.semaphore_signal(
            barrier, inc=1, device_id={"tm": t, "space": space}, device_id_type=MESH
        )

    @pl.when(has_up)
    def _():
        greet(x - 1)

    @pl.when(has_down)
    def _():
        greet(x + 1)

    own = pl.ds(0, rows)
    loads = [
        pltpu.make_async_copy(states_in.at[0], field.at[own], local_sem.at[0]),
        pltpu.make_async_copy(region_in, region.at[own], local_sem.at[1]),
        pltpu.make_async_copy(source_in, source.at[:, own], local_sem.at[2]),
    ]
    for copy in loads:
        copy.start()
    for copy in loads:
        copy.wait()
    pl.semaphore_wait(barrier, has_up.astype(jnp.int32) + has_down.astype(jnp.int32))

    def edge_copies(way):
        src = pl.ds(0, halo) if way == 0 else pl.ds(rows - halo, halo)
        dst = pl.ds(rows, halo) if way == 0 else pl.ds(up_base, halo)
        to = x - 1 if way == 0 else x + 1
        send, recv = edge_send.at[way], edge_recv.at[way]
        return [
            send_to(source.at[:, src], source.at[:, dst], send.at[2], recv.at[2], t, to),
            send_to(region.at[src], region.at[dst], send.at[0], recv.at[0], t, to),
            send_to(field.at[src], field.at[dst], send.at[1], recv.at[1], t, to),
        ]

    @pl.when(has_up)
    def _():
        for copy in edge_copies(0):
            copy.start()

    @pl.when(has_down)
    def _():
        for copy in edge_copies(1):
            copy.start()

    field_out[own] = field[own]
    region_out[own] = region[own]
    source_out[:, own] = source[:, own]

    @pl.when(has_down)
    def _():
        for copy in edge_copies(0):
            copy.wait_recv()
        at = pl.ds(rows, halo)
        field_out[at] = field[at]
        region_out[at] = region[at]
        source_out[:, at] = source[:, at]

    @pl.when(has_up)
    def _():
        for copy in edge_copies(1):
            copy.wait_recv()
        at = pl.ds(up_base, halo)
        field_out[at] = field[at]
        region_out[at] = region[at]
        source_out[:, at] = source[:, at]

    @pl.when(has_up)
    def _():
        for copy in edge_copies(0):
            copy.wait_send()

    @pl.when(has_down)
    def _():
        for copy in edge_copies(1):
            copy.wait_send()


def kernel(
    slices, strips, rows, cols, up_base, total_rows,
    begin, region, source, front_ref,
    ends_out,
    field, codes_at, coef_a, coef_b, mobile, drive,
    decay_own, decay_all, offset_own, offset_all,
    prod_own, prod_all, shift_own, shift_all, solved, end_own, end_prev,
    group_send, group_recv, level_send, level_recv,
    back_send, back_recv, halo_send, halo_recv, end_send, end_recv,
):
    t, x, level, g, levels = grid(slices)
    slab = rows // GROUP
    has_up = x > 0
    has_down = x < strips - 1
    halo = FINE
    groups = total_rows // TILE
    halves = cols // LANES

    def peer(j):
        return level * GROUP + (g + j) % GROUP

    def far(i):
        return ((level + i) % levels) * GROUP + g

    def remote(src, dst, send, recv, tm, space=None):
        return send_to(src, dst, send, recv, tm, x if space is None else space)

    barrier = pltpu.get_barrier_semaphore()

    def greet(tm, space):
        pl.semaphore_signal(
            barrier, inc=1, device_id={"tm": tm, "space": space}, device_id_type=MESH
        )

    expected = (GROUP - 1) + (levels - 1) + 2

    @pl.when(has_up)
    def _():
        for j in range(GROUP):
            greet(peer(j), x - 1)

    @pl.when(has_down)
    def _():
        for j in range(GROUP):
            greet(peer(j), x + 1)

    for j in range(1, GROUP):
        greet(peer(j), x)
    for i in range(1, levels):
        greet(far(i), x)
    greet((t + 1) % slices, x)
    greet((t + slices - 1) % slices, x)

    own = pl.ds(0, rows)
    cos0, sin0 = jnp.float32(1.0), jnp.float32(0.0)
    for b in range(max(1, (slices - 1).bit_length())):
        on = (t // (1 << b)) % 2 == 1
        angle = 2.0 * math.pi * (1 << b) / slices
        cb = jnp.where(on, jnp.float32(math.cos(angle)), jnp.float32(1.0))
        sb = jnp.where(on, jnp.float32(math.sin(angle)), jnp.float32(0.0))
        cos0, sin0 = cos0 * cb - sin0 * sb, sin0 * cb + cos0 * sb
    cos_d = math.cos(2.0 * math.pi / (slices * FINE))
    sin_d = math.sin(2.0 * math.pi / (slices * FINE))
    cut = lax.rem(front_ref[0] + (slices - 1), slices)
    keep = jnp.where(t == cut, jnp.float32(0.0), jnp.float32(1.0))

    count = expected + GROUP * (has_up.astype(jnp.int32) + has_down.astype(jnp.int32))
    sub = lax.broadcasted_iota(jnp.int32, (TILE, LANES), 0)
    lane = lax.broadcasted_iota(jnp.int32, (TILE, LANES), 1)
    top, bottom = sub == 0, sub == TILE - 1
    left, right = lane == 0, lane == LANES - 1
    own_groups = rows // TILE

    def above_and_centre(v):
        rolled = [[pltpu.roll(a, 1, 0) for a in line] for line in v]
        out = []
        for r in range(groups):
            line = []
            for h in range(halves):
                carry, centre = rolled[r - 1][h], v[r][h]
                if r == 0:
                    carry = jnp.where(has_up, carry, 0.0)
                if r == own_groups:
                    centre = jnp.where(top, jnp.where(has_down, centre, 0.0), centre)
                line.append((jnp.where(top, carry, rolled[r][h]), centre))
            out.append(line)
        return out

    def from_below(v):
        rolled = [[pltpu.roll(a, TILE - 1, 0) for a in line] for line in v]
        return [
            [jnp.where(bottom, rolled[(r + 1) % groups][h], rolled[r][h]) for h in range(halves)]
            for r in range(groups)
        ]

    def beside(even, odd):
        return (
            jnp.where(left, 0.0, pltpu.roll(odd, 1, 1)),
            jnp.where(right, 0.0, pltpu.roll(even, LANES - 1, 1)),
        )

    def place(r, h):
        return pl.ds(r * TILE, TILE), pl.ds(h * LANES, LANES)

    def tiles(ref, count):
        return [[ref[place(r, h)] for h in range(halves)] for r in range(count)]

    order = columns_apart(True)
    field[0] = moved(begin[...], order)
    codes_at[...] = moved(region[...].astype(jnp.float32), order)
    drive[0] = moved(source[0], order)
    drive[1] = moved(source[1], order)

    codes = tiles(codes_at, groups)
    relu = [[lookup(c, RELUCTIVITY) for c in line] for line in codes]
    satu = [[lookup(c, SATURATION) for c in line] for line in codes]
    relu_row, satu_row = above_and_centre(relu), above_and_centre(satu)

    def keep_face(kind, at, rels, sats):
        base = 0.5 * (rels[0] + rels[1])
        extra = base * (0.5 * (sats[0] + sats[1]))
        coef_a[kind, *at] = base + extra
        coef_b[kind, *at] = extra

    for r in range(groups):
        relu_side, satu_side = beside(*relu[r]), beside(*satu[r])
        keep_face(2, place(r, 0), relu[r], satu[r])
        for h in range(halves):
            at = place(r, h)
            keep_face(0, at, relu_row[r][h], satu_row[r][h])
            keep_face(1, at, (relu[r][h], relu_side[h]), (satu[r][h], satu_side[h]))
            move = lookup(codes[r][h], MOBILITY)
            mobile[at] = move
            drive[0, *at] = move * drive[0, *at]
            drive[1, *at] = move * drive[1, *at]

    def row_faces(v):
        weights, fluxes = [], []
        for r, line in enumerate(above_and_centre(v)):
            w, f = [], []
            for h, (above, centre) in enumerate(line):
                at = place(r, h)
                d = above - centre
                w.append(weight(d, coef_a[0, *at], coef_b[0, *at]))
                f.append(w[-1] * d)
            weights.append(w)
            fluxes.append(f)
        return weights, fluxes

    def column_faces(v, r):
        even, odd = v[r]
        at = place(r, 0)
        d = odd - even
        w = weight(d, coef_a[2, *at], coef_b[2, *at])
        out = [(w, w * d), (w, -(w * d))]
        for h, near in enumerate(beside(even, odd)):
            at = place(r, h)
            d = near - v[r][h]
            w = weight(d, coef_a[1, *at], coef_b[1, *at])
            out[h] = (out[h][0] + w, out[h][1] + w * d)
        return out

    def step(v, cos_k, sin_k):
        _, fluxes = row_faces(v)
        lower = from_below(fluxes)
        out = []
        for r in range(groups):
            line = []
            sides = column_faces(v, r)
            for h in range(halves):
                at = place(r, h)
                divergence = sides[h][1] + (fluxes[r][h] - lower[r][h])
                current = drive[0, *at] * cos_k + drive[1, *at] * sin_k
                line.append(v[r][h] + (mobile[at] * divergence + current))
            out.append(line)
        return out

    def set_decay(it, v):
        weights, _ = row_faces(v)
        lower = from_below(weights)
        for r in range(own_groups):
            sides = column_faces(v, r)
            for h in range(halves):
                at = place(r, h)
                diagonal = weights[r][h] + lower[r][h] + sides[h][0]
                decay_own[it, *at] = keep / (1.0 + FINE * mobile[at] * diagonal)

    def flat(v):
        return tuple(a for line in v for a in line)

    def nest(v):
        return [list(v[r * halves:(r + 1) * halves]) for r in range(groups)]

    mine = pl.ds(pl.multiple_of(g * slab, slab), slab)

    def group_copies(it, kind, src, dst):
        out = []
        for j in range(1, GROUP):
            to = (g + j) % GROUP
            out.append(remote(
                src.at[it, pl.ds(pl.multiple_of(to * slab, slab), slab)], dst.at[it, g],
                group_send.at[it, kind, j], group_recv.at[it, kind, g], peer(j),
            ))
        return out

    def group_wait(it, kind, dst):
        for j in range(1, GROUP):
            slot = (g + j) % GROUP
            remote(
                dst.at[it, slot], dst.at[it, slot],
                group_send.at[it, kind, j], group_recv.at[it, kind, slot], peer(j),
            ).wait_recv()

    def level_copies(it, kind, src, dst):
        return [
            remote(
                src.at[it], dst.at[it, levels - i - 1],
                level_send.at[it, kind, i], level_recv.at[it, kind, levels - i - 1], far(i),
            )
            for i in (*range(levels - 1, 0, -1),)
        ]

    def back_copies(it):
        return [
            remote(
                solved.at[it, (g + j) % GROUP], field.at[it + 1, mine],
                back_send.at[it, j], back_recv.at[it, g], peer(j),
            )
            for j in range(1, GROUP)
        ]

    def back_wait(it):
        for j in range(1, GROUP):
            slot = (g + j) % GROUP
            part = field.at[it + 1, pl.ds(pl.multiple_of(slot * slab, slab), slab)]
            remote(
                part, part, back_send.at[it, j], back_recv.at[it, slot], peer(j)
            ).wait_recv()

    per_halo = halo // slab
    low = g < per_halo
    high = g >= GROUP - per_halo

    def halo_copies(it, way):
        if way == 0:
            start, to = rows + g * slab, x - 1
        else:
            start, to = up_base + (g - (GROUP - per_halo)) * slab, x + 1
        dst = pl.ds(pl.multiple_of(start, slab), slab)
        return [
            remote(
                solved.at[it, (g + j) % GROUP], field.at[it + 1, dst],
                halo_send.at[it, way, j], halo_recv.at[it, way, g], peer(j), to,
            )
            for j in range(GROUP)
        ]

    def halo_wait(it, way):
        for k in range(per_halo):
            slot = k if way == 0 else GROUP - per_halo + k
            start = (rows if way == 0 else up_base) + k * slab
            part = field.at[it + 1, pl.ds(start, slab)]
            remote(
                part, part, halo_send.at[it, way, 0], halo_recv.at[it, way, slot],
                t, x + 1 if way == 0 else x - 1,
            ).wait_recv()

    def start_all(copies):
        for copy in copies:
            copy.start()

    def sent_all(copies):
        for copy in copies:
            copy.wait_send()

    def end_copy():
        return remote(end_own, end_prev, end_send, end_recv, (t + 1) % slices)

    def sweep(it, _):
        more = it < ITERS - 1

        def turn(k, carry):
            v, cos_k, sin_k = carry
            v = step(nest(v), cos_k, sin_k)

            @pl.when((it == 0) & (k == DECAY_AT))
            def _():
                pl.semaphore_wait(barrier, count)

            @pl.when(k == DECAY_AT)
            def _():
                start_all(group_copies(it, 0, decay_own, decay_all))
                decay_all[it, g] = decay_own[it, mine]

            @pl.when(k == PRODUCT_AT)
            def _():
                group_wait(it, 0, decay_all)
                product = decay_all[it, 0]
                for j in range(1, GROUP):
                    product = product * decay_all[it, j]
                prod_own[it] = product
                start_all(level_copies(it, 0, prod_own, prod_all))

            return flat(v), cos_k * cos_d - sin_k * sin_d, sin_k * cos_d + cos_k * sin_d

        set_decay(it, tiles(field.at[it], groups))
        v, _, _ = lax.fori_loop(0, FINE, turn, (flat(tiles(field.at[it], groups)), cos0, sin0))
        v = nest(v)
        for r in range(own_groups):
            for h in range(halves):
                at = place(r, h)
                offset_own[it, *at] = v[r][h] - decay_own[it, *at] * field[it, *at]
                end_own[at] = v[r][h]
        start_all(group_copies(it, 1, offset_own, offset_all))
        offset_all[it, g] = offset_own[it, mine]

        @pl.when(jnp.logical_not(more))
        def _():
            end_copy().start()

        group_wait(it, 1, offset_all)
        shift = offset_all[it, 0]
        for k in range(1, GROUP):
            shift = decay_all[it, k] * shift + offset_all[it, k]
        shift_own[it] = shift
        start_all(level_copies(it, 1, shift_own, shift_all))
        for copy in level_copies(it, 0, prod_own, prod_all):
            copy.wait_recv()
        value = shift
        waits = level_copies(it, 1, shift_own, shift_all)
        for r in range(levels - 1):
            waits[r].wait_recv()
            value = prod_all[it, r] * value + shift_all[it, r]
        solved[it, 0] = value
        for k in range(1, GROUP):
            value = decay_all[it, k - 1] * value + offset_all[it, k - 1]
            solved[it, k] = value
        start_all(back_copies(it))

        @pl.when(more & low & has_up)
        def _():
            start_all(halo_copies(it, 0))

        @pl.when(more & high & has_down)
        def _():
            start_all(halo_copies(it, 1))

        field[it + 1, mine] = solved[it, g]
        back_wait(it)

        @pl.when(more & has_down)
        def _():
            halo_wait(it, 0)

        @pl.when(more & has_up)
        def _():
            halo_wait(it, 1)

        sent_all(group_copies(it, 0, decay_own, decay_all))
        sent_all(group_copies(it, 1, offset_own, offset_all))
        sent_all(level_copies(it, 0, prod_own, prod_all))
        sent_all(level_copies(it, 1, shift_own, shift_all))
        sent_all(back_copies(it))

        @pl.when(more & low & has_up)
        def _():
            sent_all(halo_copies(it, 0))

        @pl.when(more & high & has_down)
        def _():
            sent_all(halo_copies(it, 1))

        return 0

    lax.fori_loop(0, ITERS, sweep, 0)

    back = columns_apart(False)
    ends_out[0] = moved(field[ITERS, own], back)
    end_copy().wait_recv()
    ends_out[1] = moved(end_prev[...], back)
    end_copy().wait_send()


def solution(mesh):
    slices, strips = mesh.shape["tm"], mesh.shape["space"]

    def on_device(start_states, region_map, source, front):
        _, rows, cols = start_states.shape
        slab = rows // GROUP
        levels = slices // GROUP
        up_base = rows if strips <= 2 else rows + FINE
        total_rows = up_base + FINE
        f32 = jnp.float32
        dma = pltpu.SemaphoreType.DMA
        vmem = pl.BlockSpec(memory_space=pltpu.VMEM)
        shapes = [
            ((total_rows, cols), f32),
            ((total_rows, cols), jnp.int32),
            ((2, total_rows, cols), f32),
        ]
        wide = pl.pallas_call(
            functools.partial(edge_kernel, strips, rows, up_base),
            out_shape=[jax.ShapeDtypeStruct(*shape) for shape in shapes],
            in_specs=[pl.BlockSpec(memory_space=pltpu.HBM)] * 3,
            out_specs=[vmem] * 3,
            scratch_shapes=[pltpu.VMEM(*shape) for shape in shapes]
            + [dma((3,)), dma((2, 3)), dma((2, 3))],
            compiler_params=pltpu.CompilerParams(
                collective_id=0, has_side_effects=True, vmem_limit_bytes=16 * 2**20
            ),
        )(*(
            pltpu.with_memory_space_constraint(a, pltpu.HBM)
            for a in (start_states, region_map, source)
        ))
        ends = pl.pallas_call(
            functools.partial(kernel, slices, strips, rows, cols, up_base, total_rows),
            out_shape=jax.ShapeDtypeStruct((2, rows, cols), f32),
            in_specs=[vmem] * 3 + [pl.BlockSpec(memory_space=pltpu.SMEM)],
            out_specs=vmem,
            scratch_shapes=[
                pltpu.VMEM((ITERS + 1, total_rows, cols), f32),
                pltpu.VMEM((total_rows, cols), f32),
                pltpu.VMEM((3, total_rows, cols), f32),
                pltpu.VMEM((3, total_rows, cols), f32),
                pltpu.VMEM((total_rows, cols), f32),
                pltpu.VMEM((2, total_rows, cols), f32),
                pltpu.VMEM((ITERS, rows, cols), f32),
                pltpu.VMEM((ITERS, GROUP, slab, cols), f32),
                pltpu.VMEM((ITERS, rows, cols), f32),
                pltpu.VMEM((ITERS, GROUP, slab, cols), f32),
                pltpu.VMEM((ITERS, slab, cols), f32),
                pltpu.VMEM((ITERS, levels - 1, slab, cols), f32),
                pltpu.VMEM((ITERS, slab, cols), f32),
                pltpu.VMEM((ITERS, levels - 1, slab, cols), f32),
                pltpu.VMEM((ITERS, GROUP, slab, cols), f32),
                pltpu.VMEM((rows, cols), f32),
                pltpu.VMEM((rows, cols), f32),
                dma((ITERS, 2, GROUP)),
                dma((ITERS, 2, GROUP)),
                dma((ITERS, 2, levels)),
                dma((ITERS, 2, levels)),
                dma((ITERS, GROUP)),
                dma((ITERS, GROUP)),
                dma((ITERS, 2, GROUP)),
                dma((ITERS, 2, GROUP)),
                dma,
                dma,
            ],
            compiler_params=pltpu.CompilerParams(
                collective_id=1, has_side_effects=True, vmem_limit_bytes=16 * 2**20
            ),
        )(*wide, jnp.reshape(front, (1,)))
        return ends[0:1], ends[1:2] - ends[0:1]

    placed = (P("tm", "space", None), P("space", None), P(None, "space", None), P())
    return jax.shard_map(
        on_device,
        mesh=mesh,
        in_specs=placed,
        out_specs=(P("tm", "space", None), P("tm", "space", None)),
        check_vma=False,
    )
```

```python
import functools
import math

import jax
import jax.numpy as jnp
from jax import lax
from jax.experimental import pallas as pl
from jax.experimental.pallas import tpu as pltpu
from jax.sharding import PartitionSpec as P

FINE = 16
ITERS = 2
GROUP = 4
DECAY_AT = 5
PRODUCT_AT = 11
TILE = 8
LANES = 128

RELUCTIVITY = (1.0, 0.3, 1.0, 0.25)
SATURATION = (0.0, 2.0, 0.0, 1.5)
MOBILITY = (0.15, 0.02, 0.0004, 0.0008)

MESH = pl.DeviceIdType.MESH


def lookup(region, table):
    result = jnp.zeros(region.shape, jnp.float32)
    for code, entry in enumerate(table):
        result = jnp.where(region == code, jnp.float32(entry), result)
    return result


def inverse(x):
    return pl.reciprocal(x, approx=True)


def grid(slices):
    t = lax.axis_index("tm")
    return t, lax.axis_index("space"), t // GROUP, t % GROUP, slices // GROUP


def send_to(src, dst, send, recv, tm, space):
    return pltpu.make_async_remote_copy(
        src_ref=src, dst_ref=dst, send_sem=send, recv_sem=recv,
        device_id={"tm": tm, "space": space}, device_id_type=MESH,
    )


def edge_kernel(
    strips, rows, up_base,
    states_in, region_in, source_in,
    field_out, region_out, source_out,
    field, region, source, local_sem, edge_send, edge_recv,
):
    t, x = lax.axis_index("tm"), lax.axis_index("space")
    has_up = x > 0
    has_down = x < strips - 1
    halo = FINE
    barrier = pltpu.get_barrier_semaphore()

    def greet(space):
        pl.semaphore_signal(
            barrier, inc=1, device_id={"tm": t, "space": space}, device_id_type=MESH
        )

    @pl.when(has_up)
    def _():
        greet(x - 1)

    @pl.when(has_down)
    def _():
        greet(x + 1)

    own = pl.ds(0, rows)
    loads = [
        pltpu.make_async_copy(states_in.at[0], field.at[own], local_sem.at[0]),
        pltpu.make_async_copy(region_in, region.at[own], local_sem.at[1]),
        pltpu.make_async_copy(source_in, source.at[:, own], local_sem.at[2]),
    ]
    for copy in loads:
        copy.start()
    for copy in loads:
        copy.wait()
    pl.semaphore_wait(barrier, has_up.astype(jnp.int32) + has_down.astype(jnp.int32))

    def edge_copies(way):
        src = pl.ds(0, halo) if way == 0 else pl.ds(rows - halo, halo)
        dst = pl.ds(rows, halo) if way == 0 else pl.ds(up_base, halo)
        to = x - 1 if way == 0 else x + 1
        send, recv = edge_send.at[way], edge_recv.at[way]
        return [
            send_to(source.at[:, src], source.at[:, dst], send.at[2], recv.at[2], t, to),
            send_to(region.at[src], region.at[dst], send.at[0], recv.at[0], t, to),
            send_to(field.at[src], field.at[dst], send.at[1], recv.at[1], t, to),
        ]

    @pl.when(has_up)
    def _():
        for copy in edge_copies(0):
            copy.start()

    @pl.when(has_down)
    def _():
        for copy in edge_copies(1):
            copy.start()

    field_out[own] = field[own]
    region_out[own] = region[own]
    source_out[:, own] = source[:, own]

    @pl.when(has_down)
    def _():
        for copy in edge_copies(0):
            copy.wait_recv()
        at = pl.ds(rows, halo)
        field_out[at] = field[at]
        region_out[at] = region[at]
        source_out[:, at] = source[:, at]

    @pl.when(has_up)
    def _():
        for copy in edge_copies(1):
            copy.wait_recv()
        at = pl.ds(up_base, halo)
        field_out[at] = field[at]
        region_out[at] = region[at]
        source_out[:, at] = source[:, at]

    @pl.when(has_up)
    def _():
        for copy in edge_copies(0):
            copy.wait_send()

    @pl.when(has_down)
    def _():
        for copy in edge_copies(1):
            copy.wait_send()


def kernel(
    slices, strips, rows, cols, up_base, total_rows,
    begin, region, source, front_ref,
    ends_out,
    field, coef_a, coef_b, drive,
    decay_own, decay_all, offset_own, offset_all,
    prod_own, prod_all, shift_own, shift_all, solved, end_own, end_prev,
    group_send, group_recv, level_send, level_recv,
    back_send, back_recv, halo_send, halo_recv, end_send, end_recv,
):
    t, x, level, g, levels = grid(slices)
    slab = rows // GROUP
    has_up = x > 0
    has_down = x < strips - 1
    halo = FINE
    groups = total_rows // TILE
    halves = cols // LANES

    def peer(j):
        return level * GROUP + (g + j) % GROUP

    def far(i):
        return ((level + i) % levels) * GROUP + g

    def remote(src, dst, send, recv, tm, space=None):
        return send_to(src, dst, send, recv, tm, x if space is None else space)

    barrier = pltpu.get_barrier_semaphore()

    def greet(tm, space):
        pl.semaphore_signal(
            barrier, inc=1, device_id={"tm": tm, "space": space}, device_id_type=MESH
        )

    expected = (GROUP - 1) + (levels - 1) + 2

    @pl.when(has_up)
    def _():
        for j in range(GROUP):
            greet(peer(j), x - 1)

    @pl.when(has_down)
    def _():
        for j in range(GROUP):
            greet(peer(j), x + 1)

    for j in range(1, GROUP):
        greet(peer(j), x)
    for i in range(1, levels):
        greet(far(i), x)
    greet((t + 1) % slices, x)
    greet((t + slices - 1) % slices, x)

    own = pl.ds(0, rows)
    cos0, sin0 = jnp.float32(1.0), jnp.float32(0.0)
    for b in range(max(1, (slices - 1).bit_length())):
        on = (t // (1 << b)) % 2 == 1
        angle = 2.0 * math.pi * (1 << b) / slices
        cb = jnp.where(on, jnp.float32(math.cos(angle)), jnp.float32(1.0))
        sb = jnp.where(on, jnp.float32(math.sin(angle)), jnp.float32(0.0))
        cos0, sin0 = cos0 * cb - sin0 * sb, sin0 * cb + cos0 * sb
    cos_d = math.cos(2.0 * math.pi / (slices * FINE))
    sin_d = math.sin(2.0 * math.pi / (slices * FINE))
    cut = lax.rem(front_ref[0] + (slices - 1), slices)
    keep = jnp.where(t == cut, jnp.float32(0.0), jnp.float32(1.0))

    count = expected + GROUP * (has_up.astype(jnp.int32) + has_down.astype(jnp.int32))
    sub = lax.broadcasted_iota(jnp.int32, (TILE, LANES), 0)
    lane = lax.broadcasted_iota(jnp.int32, (TILE, LANES), 1)
    top, bottom = sub == 0, sub == TILE - 1
    left, right = lane == 0, lane == LANES - 1
    own_groups = rows // TILE

    def neighbours(v):
        down_roll = [[pltpu.roll(a, 1, 0) for a in line] for line in v]
        up_roll = [[pltpu.roll(a, TILE - 1, 0) for a in line] for line in v]
        right_roll = [[pltpu.roll(a, 1, 1) for a in line] for line in v]
        left_roll = [[pltpu.roll(a, LANES - 1, 1) for a in line] for line in v]
        out = []
        for r in range(groups):
            line = []
            for h in range(halves):
                above = down_roll[r - 1][h]
                if r == 0:
                    above = jnp.where(has_up, above, 0.0)
                below = up_roll[(r + 1) % groups][h]
                if r == own_groups - 1:
                    below = jnp.where(has_down, below, 0.0)
                before = right_roll[r][h - 1] if h > 0 else 0.0
                after = left_roll[r][h + 1] if h < halves - 1 else 0.0
                line.append((
                    jnp.where(top, above, down_roll[r][h]),
                    jnp.where(bottom, below, up_roll[r][h]),
                    jnp.where(left, before, right_roll[r][h]),
                    jnp.where(right, after, left_roll[r][h]),
                ))
            out.append(line)
        return out

    def place(r, h):
        return pl.ds(r * TILE, TILE), pl.ds(h * LANES, LANES)

    def tiles(ref, count):
        return [[ref[place(r, h)] for h in range(halves)] for r in range(count)]

    codes = tiles(region, groups)
    relu = [[lookup(c, RELUCTIVITY) for c in line] for line in codes]
    satu = [[lookup(c, SATURATION) for c in line] for line in codes]
    relu_near, satu_near = neighbours(relu), neighbours(satu)
    for r in range(groups):
        for h in range(halves):
            mobile = lookup(codes[r][h], MOBILITY)
            at = place(r, h)
            for f in range(4):
                face_rel = 0.5 * (relu[r][h] + relu_near[r][h][f])
                face_sat = 0.5 * (satu[r][h] + satu_near[r][h][f])
                base = mobile * face_rel
                coef_b[f, *at] = base * face_sat
                coef_a[f, *at] = base + base * face_sat
            drive[0, *at] = mobile * source[0, *at]
            drive[1, *at] = mobile * source[1, *at]

    def step(v, cos_k, sin_k):
        near = neighbours(v)
        out, diagonals = [], []
        for r in range(groups):
            line, diag_line = [], []
            for h in range(halves):
                at = place(r, h)
                c = v[r][h]
                gain = drive[0, *at] * cos_k + drive[1, *at] * sin_k
                diagonal = None
                for f in range(4):
                    d = near[r][h][f] - c
                    q = coef_a[f, *at] - coef_b[f, *at] * inverse(1.0 + d * d)
                    gain = gain + q * d
                    diagonal = q if diagonal is None else diagonal + q
                line.append(c + gain)
                diag_line.append(diagonal)
            out.append(line)
            diagonals.append(diag_line)
        return out, diagonals

    def flat(v):
        return tuple(a for line in v for a in line)

    def nest(v):
        return [list(v[r * halves:(r + 1) * halves]) for r in range(groups)]

    mine = pl.ds(pl.multiple_of(g * slab, slab), slab)

    def group_copies(it, kind, src, dst):
        out = []
        for j in (2, 3, 1):
            to = (g + j) % GROUP
            out.append(remote(
                src.at[it, pl.ds(pl.multiple_of(to * slab, slab), slab)], dst.at[it, g],
                group_send.at[it, kind], group_recv.at[it, kind], peer(j),
            ))
        return out

    def group_all(it, kind, dst):
        part = dst.at[it, pl.ds(0, GROUP - 1)]
        return remote(part, part, group_send.at[it, kind], group_recv.at[it, kind], peer(1))

    def level_copies(it, kind, src, dst):
        return [
            remote(
                src.at[it], dst.at[it, levels - i - 1],
                level_send.at[it, kind], level_recv.at[it, kind], far(i),
            )
            for i in range(levels - 1, 0, -1)
        ]

    def level_all(it, kind, dst):
        part = dst.at[it]
        return remote(part, part, level_send.at[it, kind], level_recv.at[it, kind], far(1))

    def back_copies(it):
        return [
            remote(
                solved.at[it, (g + j) % GROUP], field.at[it + 1, mine],
                back_send.at[it], back_recv.at[it], peer(j),
            )
            for j in (2, 3, 1)
        ]

    def back_all(it):
        part = solved.at[it, pl.ds(0, GROUP - 1)]
        return remote(part, part, back_send.at[it], back_recv.at[it], peer(1))

    per_halo = halo // slab
    low = g < per_halo
    high = g >= GROUP - per_halo

    def halo_copies(it, way):
        if way == 0:
            start, to = rows + g * slab, x - 1
        else:
            start, to = up_base + (g - (GROUP - per_halo)) * slab, x + 1
        dst = pl.ds(pl.multiple_of(start, slab), slab)
        return [
            remote(
                solved.at[it, (g + j) % GROUP], field.at[it + 1, dst],
                halo_send.at[it, way], halo_recv.at[it, way], peer(j), to,
            )
            for j in (2, 3, 1, 0)
        ]

    def halo_sent(it, way):
        part = solved.at[it]
        return remote(part, part, halo_send.at[it, way], halo_recv.at[it, way], peer(1))

    def halo_here(it, way):
        part = field.at[it + 1, pl.ds(rows if way == 0 else up_base, halo)]
        return remote(part, part, halo_send.at[it, way], halo_recv.at[it, way], peer(1))

    def start_all(copies):
        for copy in copies:
            copy.start()

    def end_copy():
        return remote(end_own, end_prev, end_send, end_recv, (t + 1) % slices)

    for r in range(groups):
        for h in range(halves):
            field[0, *place(r, h)] = begin[place(r, h)]

    def sweep(it, _):
        more = it < ITERS - 1

        def turn(k, carry):
            v, cos_k, sin_k = carry
            v, diagonals = step(nest(v), cos_k, sin_k)

            @pl.when(k == 0)
            def _():
                for r in range(own_groups):
                    for h in range(halves):
                        decay_own[it, *place(r, h)] = keep / (1.0 + FINE * diagonals[r][h])

            @pl.when((it == 0) & (k == DECAY_AT))
            def _():
                pl.semaphore_wait(barrier, count)

            @pl.when(k == DECAY_AT)
            def _():
                start_all(group_copies(it, 0, decay_own, decay_all))
                decay_all[it, g] = decay_own[it, mine]

            @pl.when(k == PRODUCT_AT)
            def _():
                group_all(it, 0, decay_all).wait_recv()
                product = decay_all[it, 0]
                for j in range(1, GROUP):
                    product = product * decay_all[it, j]
                prod_own[it] = product
                start_all(level_copies(it, 0, prod_own, prod_all))

            return flat(v), cos_k * cos_d - sin_k * sin_d, sin_k * cos_d + cos_k * sin_d

        v, _, _ = lax.fori_loop(0, FINE, turn, (flat(tiles(field.at[it], groups)), cos0, sin0))
        v = nest(v)
        for r in range(own_groups):
            for h in range(halves):
                at = place(r, h)
                offset_own[it, *at] = v[r][h] - decay_own[it, *at] * field[it, *at]
                end_own[at] = v[r][h]
        start_all(group_copies(it, 1, offset_own, offset_all))
        offset_all[it, g] = offset_own[it, mine]

        @pl.when(jnp.logical_not(more))
        def _():
            end_copy().start()

        group_all(it, 1, offset_all).wait_recv()
        shift = offset_all[it, 0]
        for k in range(1, GROUP):
            shift = decay_all[it, k] * shift + offset_all[it, k]
        shift_own[it] = shift
        start_all(level_copies(it, 1, shift_own, shift_all))
        level_all(it, 0, prod_all).wait_recv()
        level_all(it, 1, shift_all).wait_recv()
        value = shift
        for r in range(levels - 1):
            value = prod_all[it, r] * value + shift_all[it, r]
        solved[it, 0] = value
        for k in range(1, GROUP):
            value = decay_all[it, k - 1] * value + offset_all[it, k - 1]
            solved[it, k] = value
        @pl.when(more & low & has_up)
        def _():
            start_all(halo_copies(it, 0))

        @pl.when(more & high & has_down)
        def _():
            start_all(halo_copies(it, 1))

        start_all(back_copies(it))
        field[it + 1, mine] = solved[it, g]
        back_all(it).wait_recv()

        @pl.when(more & has_down)
        def _():
            halo_here(it, 0).wait_recv()

        @pl.when(more & has_up)
        def _():
            halo_here(it, 1).wait_recv()

        group_all(it, 0, decay_all).wait_send()
        group_all(it, 1, offset_all).wait_send()
        level_all(it, 0, prod_all).wait_send()
        level_all(it, 1, shift_all).wait_send()
        back_all(it).wait_send()

        @pl.when(more & low & has_up)
        def _():
            halo_sent(it, 0).wait_send()

        @pl.when(more & high & has_down)
        def _():
            halo_sent(it, 1).wait_send()

        return 0

    lax.fori_loop(0, ITERS, sweep, 0)

    ends_out[0] = field[ITERS, own]
    end_copy().wait_recv()
    ends_out[1] = end_prev[...]
    end_copy().wait_send()


def solution(mesh):
    slices, strips = mesh.shape["tm"], mesh.shape["space"]

    def on_device(start_states, region_map, source, front):
        _, rows, cols = start_states.shape
        slab = rows // GROUP
        levels = slices // GROUP
        up_base = rows if strips <= 2 else rows + FINE
        total_rows = up_base + FINE
        f32 = jnp.float32
        dma = pltpu.SemaphoreType.DMA
        vmem = pl.BlockSpec(memory_space=pltpu.VMEM)
        shapes = [
            ((total_rows, cols), f32),
            ((total_rows, cols), jnp.int32),
            ((2, total_rows, cols), f32),
        ]
        wide = pl.pallas_call(
            functools.partial(edge_kernel, strips, rows, up_base),
            out_shape=[jax.ShapeDtypeStruct(*shape) for shape in shapes],
            in_specs=[pl.BlockSpec(memory_space=pltpu.HBM)] * 3,
            out_specs=[vmem] * 3,
            scratch_shapes=[pltpu.VMEM(*shape) for shape in shapes]
            + [dma((3,)), dma((2, 3)), dma((2, 3))],
            compiler_params=pltpu.CompilerParams(
                collective_id=0, has_side_effects=True, vmem_limit_bytes=16 * 2**20
            ),
        )(*(
            pltpu.with_memory_space_constraint(a, pltpu.HBM)
            for a in (start_states, region_map, source)
        ))
        ends = pl.pallas_call(
            functools.partial(kernel, slices, strips, rows, cols, up_base, total_rows),
            out_shape=jax.ShapeDtypeStruct((2, rows, cols), f32),
            in_specs=[vmem] * 3 + [pl.BlockSpec(memory_space=pltpu.SMEM)],
            out_specs=vmem,
            scratch_shapes=[
                pltpu.VMEM((ITERS + 1, total_rows, cols), f32),
                pltpu.VMEM((4, total_rows, cols), f32),
                pltpu.VMEM((4, total_rows, cols), f32),
                pltpu.VMEM((2, total_rows, cols), f32),
                pltpu.VMEM((ITERS, rows, cols), f32),
                pltpu.VMEM((ITERS, GROUP, slab, cols), f32),
                pltpu.VMEM((ITERS, rows, cols), f32),
                pltpu.VMEM((ITERS, GROUP, slab, cols), f32),
                pltpu.VMEM((ITERS, slab, cols), f32),
                pltpu.VMEM((ITERS, levels - 1, slab, cols), f32),
                pltpu.VMEM((ITERS, slab, cols), f32),
                pltpu.VMEM((ITERS, levels - 1, slab, cols), f32),
                pltpu.VMEM((ITERS, GROUP, slab, cols), f32),
                pltpu.VMEM((rows, cols), f32),
                pltpu.VMEM((rows, cols), f32),
                dma((ITERS, 2)),
                dma((ITERS, 2)),
                dma((ITERS, 2)),
                dma((ITERS, 2)),
                dma((ITERS,)),
                dma((ITERS,)),
                dma((ITERS, 2)),
                dma((ITERS, 2)),
                dma,
                dma,
            ],
            compiler_params=pltpu.CompilerParams(
                collective_id=1, has_side_effects=True, vmem_limit_bytes=16 * 2**20
            ),
        )(*wide, jnp.reshape(front, (1,)))
        return ends[0:1], ends[1:2] - ends[0:1]

    placed = (P("tm", "space", None), P("space", None), P(None, "space", None), P())
    return jax.shard_map(
        on_device,
        mesh=mesh,
        in_specs=placed,
        out_specs=(P("tm", "space", None), P("tm", "space", None)),
        check_vma=False,
    )
```

```python
import functools
import math

import jax
import jax.numpy as jnp
from jax import lax
from jax.experimental import pallas as pl
from jax.experimental.pallas import tpu as pltpu
from jax.sharding import PartitionSpec as P

FINE = 16
ITERS = 2
GROUP = 4
PAIR = 2
DECAY_AT = 2
PRODUCT_AT = 5
TILE = 8
LANES = 128

RELUCTIVITY = (1.0, 0.3, 1.0, 0.25)
SATURATION = (0.0, 2.0, 0.0, 1.5)
MOBILITY = (0.15, 0.02, 0.0004, 0.0008)

MESH = pl.DeviceIdType.MESH


def lookup(region, table):
    result = jnp.zeros(region.shape, jnp.float32)
    for code, entry in enumerate(table):
        result = jnp.where(region == code, jnp.float32(entry), result)
    return result


def inverse(x):
    return pl.reciprocal(x, approx=True)


def grid(slices):
    t = lax.axis_index("tm")
    return t, lax.axis_index("space"), t // GROUP, t % GROUP, slices // GROUP


def send_to(src, dst, send, recv, tm, space):
    return pltpu.make_async_remote_copy(
        src_ref=src, dst_ref=dst, send_sem=send, recv_sem=recv,
        device_id={"tm": tm, "space": space}, device_id_type=MESH,
    )


def edge_kernel(
    strips, rows, up_base,
    states_in, region_in, source_in,
    field_out, region_out, source_out,
    field, region, source, local_sem, edge_send, edge_recv,
):
    t, x = lax.axis_index("tm"), lax.axis_index("space")
    has_up = x > 0
    has_down = x < strips - 1
    halo = FINE
    barrier = pltpu.get_barrier_semaphore()

    def greet(space):
        pl.semaphore_signal(
            barrier, inc=1, device_id={"tm": t, "space": space}, device_id_type=MESH
        )

    @pl.when(has_up)
    def _():
        greet(x - 1)

    @pl.when(has_down)
    def _():
        greet(x + 1)

    own = pl.ds(0, rows)
    loads = [
        pltpu.make_async_copy(states_in.at[0], field.at[own], local_sem.at[0]),
        pltpu.make_async_copy(region_in, region.at[own], local_sem.at[1]),
        pltpu.make_async_copy(source_in, source.at[:, own], local_sem.at[2]),
    ]
    for copy in loads:
        copy.start()
    for copy in loads:
        copy.wait()
    pl.semaphore_wait(barrier, has_up.astype(jnp.int32) + has_down.astype(jnp.int32))

    def edge_copies(way):
        src = pl.ds(0, halo) if way == 0 else pl.ds(rows - halo, halo)
        dst = pl.ds(rows, halo) if way == 0 else pl.ds(up_base, halo)
        to = x - 1 if way == 0 else x + 1
        send, recv = edge_send.at[way], edge_recv.at[way]
        return [
            send_to(source.at[:, src], source.at[:, dst], send.at[2], recv.at[2], t, to),
            send_to(region.at[src], region.at[dst], send.at[0], recv.at[0], t, to),
            send_to(field.at[src], field.at[dst], send.at[1], recv.at[1], t, to),
        ]

    @pl.when(has_up)
    def _():
        for copy in edge_copies(0):
            copy.start()

    @pl.when(has_down)
    def _():
        for copy in edge_copies(1):
            copy.start()

    field_out[own] = field[own]
    region_out[own] = region[own]
    source_out[:, own] = source[:, own]

    @pl.when(has_down)
    def _():
        for copy in edge_copies(0):
            copy.wait_recv()
        at = pl.ds(rows, halo)
        field_out[at] = field[at]
        region_out[at] = region[at]
        source_out[:, at] = source[:, at]

    @pl.when(has_up)
    def _():
        for copy in edge_copies(1):
            copy.wait_recv()
        at = pl.ds(up_base, halo)
        field_out[at] = field[at]
        region_out[at] = region[at]
        source_out[:, at] = source[:, at]

    @pl.when(has_up)
    def _():
        for copy in edge_copies(0):
            copy.wait_send()

    @pl.when(has_down)
    def _():
        for copy in edge_copies(1):
            copy.wait_send()


def kernel(
    slices, strips, rows, cols, up_base, total_rows,
    begin, region, source, front_ref,
    ends_out,
    field, coef_a, coef_b, drive,
    decay_own, decay_all, offset_own, offset_all,
    prod_own, prod_all, shift_own, shift_all, solved, end_own, end_prev,
    group_send, group_recv, level_send, level_recv,
    back_send, back_recv, halo_send, halo_recv, end_send, end_recv,
):
    t, x, level, g, levels = grid(slices)
    slab = rows // GROUP
    has_up = x > 0
    has_down = x < strips - 1
    halo = FINE
    groups = total_rows // TILE
    halves = cols // LANES

    def peer(j):
        return level * GROUP + (g + j) % GROUP

    def far(i):
        return ((level + i) % levels) * GROUP + g

    def remote(src, dst, send, recv, tm, space=None):
        return send_to(src, dst, send, recv, tm, x if space is None else space)

    barrier = pltpu.get_barrier_semaphore()

    def greet(tm, space):
        pl.semaphore_signal(
            barrier, inc=1, device_id={"tm": tm, "space": space}, device_id_type=MESH
        )

    expected = (GROUP - 1) + (levels - 1) + 2

    @pl.when(has_up)
    def _():
        for j in range(GROUP):
            greet(peer(j), x - 1)

    @pl.when(has_down)
    def _():
        for j in range(GROUP):
            greet(peer(j), x + 1)

    for j in range(1, GROUP):
        greet(peer(j), x)
    for i in range(1, levels):
        greet(far(i), x)
    greet((t + 1) % slices, x)
    greet((t + slices - 1) % slices, x)

    own = pl.ds(0, rows)
    cos0, sin0 = jnp.float32(1.0), jnp.float32(0.0)
    for b in range(max(1, (slices - 1).bit_length())):
        on = (t // (1 << b)) % 2 == 1
        angle = 2.0 * math.pi * (1 << b) / slices
        cb = jnp.where(on, jnp.float32(math.cos(angle)), jnp.float32(1.0))
        sb = jnp.where(on, jnp.float32(math.sin(angle)), jnp.float32(0.0))
        cos0, sin0 = cos0 * cb - sin0 * sb, sin0 * cb + cos0 * sb
    cos_d = math.cos(2.0 * math.pi / (slices * FINE))
    sin_d = math.sin(2.0 * math.pi / (slices * FINE))
    cut = lax.rem(front_ref[0] + (slices - 1), slices)
    keep = jnp.where(t == cut, jnp.float32(0.0), jnp.float32(1.0))

    count = expected + GROUP * (has_up.astype(jnp.int32) + has_down.astype(jnp.int32))
    sub = lax.broadcasted_iota(jnp.int32, (TILE, LANES), 0)
    lane = lax.broadcasted_iota(jnp.int32, (TILE, LANES), 1)
    top, bottom = sub == 0, sub == TILE - 1
    left, right = lane == 0, lane == LANES - 1
    own_groups = rows // TILE

    def neighbours(v):
        down_roll = [[pltpu.roll(a, 1, 0) for a in line] for line in v]
        up_roll = [[pltpu.roll(a, TILE - 1, 0) for a in line] for line in v]
        right_roll = [[pltpu.roll(a, 1, 1) for a in line] for line in v]
        left_roll = [[pltpu.roll(a, LANES - 1, 1) for a in line] for line in v]
        out = []
        for r in range(groups):
            line = []
            for h in range(halves):
                above = down_roll[r - 1][h]
                if r == 0:
                    above = jnp.where(has_up, above, 0.0)
                below = up_roll[(r + 1) % groups][h]
                if r == own_groups - 1:
                    below = jnp.where(has_down, below, 0.0)
                before = right_roll[r][h - 1] if h > 0 else 0.0
                after = left_roll[r][h + 1] if h < halves - 1 else 0.0
                line.append((
                    jnp.where(top, above, down_roll[r][h]),
                    jnp.where(bottom, below, up_roll[r][h]),
                    jnp.where(left, before, right_roll[r][h]),
                    jnp.where(right, after, left_roll[r][h]),
                ))
            out.append(line)
        return out

    def place(r, h):
        return pl.ds(r * TILE, TILE), pl.ds(h * LANES, LANES)

    def tiles(ref, count):
        return [[ref[place(r, h)] for h in range(halves)] for r in range(count)]

    codes = tiles(region, groups)
    relu = [[lookup(c, RELUCTIVITY) for c in line] for line in codes]
    satu = [[lookup(c, SATURATION) for c in line] for line in codes]
    relu_near, satu_near = neighbours(relu), neighbours(satu)
    for r in range(groups):
        for h in range(halves):
            mobile = lookup(codes[r][h], MOBILITY)
            at = place(r, h)
            for f in range(4):
                face_rel = 0.5 * (relu[r][h] + relu_near[r][h][f])
                face_sat = 0.5 * (satu[r][h] + satu_near[r][h][f])
                base = mobile * face_rel
                coef_b[f, *at] = base * face_sat
                coef_a[f, *at] = base + base * face_sat
            drive[0, *at] = mobile * source[0, *at]
            drive[1, *at] = mobile * source[1, *at]

    def step(v, cos_k, sin_k):
        near = neighbours(v)
        out, diagonals = [], []
        for r in range(groups):
            line, diag_line = [], []
            for h in range(halves):
                at = place(r, h)
                c = v[r][h]
                gain = drive[0, *at] * cos_k + drive[1, *at] * sin_k
                diagonal = None
                for f in range(4):
                    d = near[r][h][f] - c
                    q = coef_a[f, *at] - coef_b[f, *at] * inverse(1.0 + d * d)
                    gain = gain + q * d
                    diagonal = q if diagonal is None else diagonal + q
                line.append(c + gain)
                diag_line.append(diagonal)
            out.append(line)
            diagonals.append(diag_line)
        return out, diagonals

    def flat(v):
        return tuple(a for line in v for a in line)

    def nest(v):
        return [list(v[r * halves:(r + 1) * halves]) for r in range(groups)]

    mine = pl.ds(pl.multiple_of(g * slab, slab), slab)

    def group_copies(it, kind, src, dst):
        out = []
        for j in (2, 3, 1):
            to = (g + j) % GROUP
            out.append(remote(
                src.at[it, pl.ds(pl.multiple_of(to * slab, slab), slab)], dst.at[it, g],
                group_send.at[it, kind], group_recv.at[it, kind], peer(j),
            ))
        return out

    def group_all(it, kind, dst):
        part = dst.at[it, pl.ds(0, GROUP - 1)]
        return remote(part, part, group_send.at[it, kind], group_recv.at[it, kind], peer(1))

    def level_copies(it, kind, src, dst):
        return [
            remote(
                src.at[it], dst.at[it, levels - i - 1],
                level_send.at[it, kind], level_recv.at[it, kind], far(i),
            )
            for i in range(levels - 1, 0, -1)
        ]

    def level_all(it, kind, dst):
        part = dst.at[it]
        return remote(part, part, level_send.at[it, kind], level_recv.at[it, kind], far(1))

    def back_copies(it):
        return [
            remote(
                solved.at[it, (g + j) % GROUP], field.at[it + 1, mine],
                back_send.at[it], back_recv.at[it], peer(j),
            )
            for j in (2, 3, 1)
        ]

    def back_all(it):
        part = solved.at[it, pl.ds(0, GROUP - 1)]
        return remote(part, part, back_send.at[it], back_recv.at[it], peer(1))

    per_halo = halo // slab
    low = g < per_halo
    high = g >= GROUP - per_halo

    def halo_copies(it, way):
        if way == 0:
            start, to = rows + g * slab, x - 1
        else:
            start, to = up_base + (g - (GROUP - per_halo)) * slab, x + 1
        dst = pl.ds(pl.multiple_of(start, slab), slab)
        return [
            remote(
                solved.at[it, (g + j) % GROUP], field.at[it + 1, dst],
                halo_send.at[it, way], halo_recv.at[it, way], peer(j), to,
            )
            for j in (2, 3, 1, 0)
        ]

    def halo_sent(it, way):
        part = solved.at[it]
        return remote(part, part, halo_send.at[it, way], halo_recv.at[it, way], peer(1))

    def halo_here(it, way):
        part = field.at[it + 1, pl.ds(rows if way == 0 else up_base, halo)]
        return remote(part, part, halo_send.at[it, way], halo_recv.at[it, way], peer(1))

    def start_all(copies):
        for copy in copies:
            copy.start()

    def end_copy():
        return remote(end_own, end_prev, end_send, end_recv, (t + 1) % slices)

    for r in range(groups):
        for h in range(halves):
            field[0, *place(r, h)] = begin[place(r, h)]

    def sweep(it, _):
        more = it < ITERS - 1

        def turn(k, carry):
            v, cos_k, sin_k = carry
            v, diagonals = step(nest(v), cos_k, sin_k)
            for _ in range(1, PAIR):
                cos_k, sin_k = cos_k * cos_d - sin_k * sin_d, sin_k * cos_d + cos_k * sin_d
                v, _ = step(v, cos_k, sin_k)

            @pl.when(k == 0)
            def _():
                for r in range(own_groups):
                    for h in range(halves):
                        decay_own[it, *place(r, h)] = keep / (1.0 + FINE * diagonals[r][h])

            @pl.when((it == 0) & (k == DECAY_AT))
            def _():
                pl.semaphore_wait(barrier, count)

            @pl.when(k == DECAY_AT)
            def _():
                start_all(group_copies(it, 0, decay_own, decay_all))
                decay_all[it, g] = decay_own[it, mine]

            @pl.when(k == PRODUCT_AT)
            def _():
                group_all(it, 0, decay_all).wait_recv()
                product = decay_all[it, 0]
                for j in range(1, GROUP):
                    product = product * decay_all[it, j]
                prod_own[it] = product
                start_all(level_copies(it, 0, prod_own, prod_all))

            return flat(v), cos_k * cos_d - sin_k * sin_d, sin_k * cos_d + cos_k * sin_d

        v, _, _ = lax.fori_loop(0, FINE // PAIR, turn, (flat(tiles(field.at[it], groups)), cos0, sin0))
        v = nest(v)
        for r in range(own_groups):
            for h in range(halves):
                at = place(r, h)
                offset_own[it, *at] = v[r][h] - decay_own[it, *at] * field[it, *at]
                end_own[at] = v[r][h]
        start_all(group_copies(it, 1, offset_own, offset_all))
        offset_all[it, g] = offset_own[it, mine]

        @pl.when(jnp.logical_not(more))
        def _():
            end_copy().start()

        group_all(it, 1, offset_all).wait_recv()
        shift = offset_all[it, 0]
        for k in range(1, GROUP):
            shift = decay_all[it, k] * shift + offset_all[it, k]
        shift_own[it] = shift
        start_all(level_copies(it, 1, shift_own, shift_all))
        level_all(it, 0, prod_all).wait_recv()
        level_all(it, 1, shift_all).wait_recv()
        value = shift
        for r in range(levels - 1):
            value = prod_all[it, r] * value + shift_all[it, r]
        solved[it, 0] = value
        for k in range(1, GROUP):
            value = decay_all[it, k - 1] * value + offset_all[it, k - 1]
            solved[it, k] = value
        @pl.when(more & low & has_up)
        def _():
            start_all(halo_copies(it, 0))

        @pl.when(more & high & has_down)
        def _():
            start_all(halo_copies(it, 1))

        start_all(back_copies(it))
        field[it + 1, mine] = solved[it, g]
        back_all(it).wait_recv()

        @pl.when(more & has_down)
        def _():
            halo_here(it, 0).wait_recv()

        @pl.when(more & has_up)
        def _():
            halo_here(it, 1).wait_recv()

        return 0

    lax.fori_loop(0, ITERS, sweep, 0)

    ends_out[0] = field[ITERS, own]
    end_copy().wait_recv()
    ends_out[1] = end_prev[...]
    end_copy().wait_send()

    def settle(it, _):
        more = it < ITERS - 1
        group_all(it, 0, decay_all).wait_send()
        group_all(it, 1, offset_all).wait_send()
        level_all(it, 0, prod_all).wait_send()
        level_all(it, 1, shift_all).wait_send()
        back_all(it).wait_send()

        @pl.when(more & low & has_up)
        def _():
            halo_sent(it, 0).wait_send()

        @pl.when(more & high & has_down)
        def _():
            halo_sent(it, 1).wait_send()

        return 0

    lax.fori_loop(0, ITERS, settle, 0)


def solution(mesh):
    slices, strips = mesh.shape["tm"], mesh.shape["space"]

    def on_device(start_states, region_map, source, front):
        _, rows, cols = start_states.shape
        slab = rows // GROUP
        levels = slices // GROUP
        up_base = rows if strips <= 2 else rows + FINE
        total_rows = up_base + FINE
        f32 = jnp.float32
        dma = pltpu.SemaphoreType.DMA
        vmem = pl.BlockSpec(memory_space=pltpu.VMEM)
        shapes = [
            ((total_rows, cols), f32),
            ((total_rows, cols), jnp.int32),
            ((2, total_rows, cols), f32),
        ]
        wide = pl.pallas_call(
            functools.partial(edge_kernel, strips, rows, up_base),
            out_shape=[jax.ShapeDtypeStruct(*shape) for shape in shapes],
            in_specs=[pl.BlockSpec(memory_space=pltpu.HBM)] * 3,
            out_specs=[vmem] * 3,
            scratch_shapes=[pltpu.VMEM(*shape) for shape in shapes]
            + [dma((3,)), dma((2, 3)), dma((2, 3))],
            compiler_params=pltpu.CompilerParams(
                collective_id=0, has_side_effects=True, vmem_limit_bytes=16 * 2**20
            ),
        )(*(
            pltpu.with_memory_space_constraint(a, pltpu.HBM)
            for a in (start_states, region_map, source)
        ))
        ends = pl.pallas_call(
            functools.partial(kernel, slices, strips, rows, cols, up_base, total_rows),
            out_shape=jax.ShapeDtypeStruct((2, rows, cols), f32),
            in_specs=[vmem] * 3 + [pl.BlockSpec(memory_space=pltpu.SMEM)],
            out_specs=vmem,
            scratch_shapes=[
                pltpu.VMEM((ITERS + 1, total_rows, cols), f32),
                pltpu.VMEM((4, total_rows, cols), f32),
                pltpu.VMEM((4, total_rows, cols), f32),
                pltpu.VMEM((2, total_rows, cols), f32),
                pltpu.VMEM((ITERS, rows, cols), f32),
                pltpu.VMEM((ITERS, GROUP, slab, cols), f32),
                pltpu.VMEM((ITERS, rows, cols), f32),
                pltpu.VMEM((ITERS, GROUP, slab, cols), f32),
                pltpu.VMEM((ITERS, slab, cols), f32),
                pltpu.VMEM((ITERS, levels - 1, slab, cols), f32),
                pltpu.VMEM((ITERS, slab, cols), f32),
                pltpu.VMEM((ITERS, levels - 1, slab, cols), f32),
                pltpu.VMEM((ITERS, GROUP, slab, cols), f32),
                pltpu.VMEM((rows, cols), f32),
                pltpu.VMEM((rows, cols), f32),
                dma((ITERS, 2)),
                dma((ITERS, 2)),
                dma((ITERS, 2)),
                dma((ITERS, 2)),
                dma((ITERS,)),
                dma((ITERS,)),
                dma((ITERS, 2)),
                dma((ITERS, 2)),
                dma,
                dma,
            ],
            compiler_params=pltpu.CompilerParams(
                collective_id=1, has_side_effects=True, vmem_limit_bytes=16 * 2**20
            ),
        )(*wide, jnp.reshape(front, (1,)))
        return ends[0:1], ends[1:2] - ends[0:1]

    placed = (P("tm", "space", None), P("space", None), P(None, "space", None), P())
    return jax.shard_map(
        on_device,
        mesh=mesh,
        in_specs=placed,
        out_specs=(P("tm", "space", None), P("tm", "space", None)),
        check_vma=False,
    )
```

```python
import functools
import math

import jax
import jax.numpy as jnp
from jax import lax
from jax.experimental import pallas as pl
from jax.experimental.pallas import tpu as pltpu
from jax.sharding import PartitionSpec as P

FINE = 16
ITERS = 2
GROUP = 4
PAIR = 2
DECAY_AT = 4
PRODUCT_AT = 6
TILE = 8
LANES = 128

RELUCTIVITY = (1.0, 0.3, 1.0, 0.25)
SATURATION = (0.0, 2.0, 0.0, 1.5)
MOBILITY = (0.15, 0.02, 0.0004, 0.0008)

MESH = pl.DeviceIdType.MESH


def lookup(region, table):
    result = jnp.zeros(region.shape, jnp.float32)
    for code, entry in enumerate(table):
        result = jnp.where(region == code, jnp.float32(entry), result)
    return result


def inverse(x):
    return pl.reciprocal(x, approx=True)


def grid(slices):
    t = lax.axis_index("tm")
    return t, lax.axis_index("space"), t // GROUP, t % GROUP, slices // GROUP


def send_to(src, dst, send, recv, tm, space):
    return pltpu.make_async_remote_copy(
        src_ref=src, dst_ref=dst, send_sem=send, recv_sem=recv,
        device_id={"tm": tm, "space": space}, device_id_type=MESH,
    )


def edge_kernel(
    strips, rows, up_base,
    states_in, region_in, source_in,
    field_out, region_out, source_out,
    field, region, source, local_sem, edge_send, edge_recv,
):
    t, x = lax.axis_index("tm"), lax.axis_index("space")
    has_up = x > 0
    has_down = x < strips - 1
    halo = FINE
    barrier = pltpu.get_barrier_semaphore()

    def greet(space):
        pl.semaphore_signal(
            barrier, inc=1, device_id={"tm": t, "space": space}, device_id_type=MESH
        )

    @pl.when(has_up)
    def _():
        greet(x - 1)

    @pl.when(has_down)
    def _():
        greet(x + 1)

    own = pl.ds(0, rows)
    loads = [
        pltpu.make_async_copy(states_in.at[0], field.at[own], local_sem.at[0]),
        pltpu.make_async_copy(region_in, region.at[own], local_sem.at[1]),
        pltpu.make_async_copy(source_in, source.at[:, own], local_sem.at[2]),
    ]
    for copy in loads:
        copy.start()
    for copy in loads:
        copy.wait()
    pl.semaphore_wait(barrier, has_up.astype(jnp.int32) + has_down.astype(jnp.int32))

    def edge_copies(way):
        src = pl.ds(0, halo) if way == 0 else pl.ds(rows - halo, halo)
        dst = pl.ds(rows, halo) if way == 0 else pl.ds(up_base, halo)
        to = x - 1 if way == 0 else x + 1
        send, recv = edge_send.at[way], edge_recv.at[way]
        return [
            send_to(source.at[:, src], source.at[:, dst], send.at[2], recv.at[2], t, to),
            send_to(region.at[src], region.at[dst], send.at[0], recv.at[0], t, to),
            send_to(field.at[src], field.at[dst], send.at[1], recv.at[1], t, to),
        ]

    @pl.when(has_up)
    def _():
        for copy in edge_copies(0):
            copy.start()

    @pl.when(has_down)
    def _():
        for copy in edge_copies(1):
            copy.start()

    field_out[own] = field[own]
    region_out[own] = region[own]
    source_out[:, own] = source[:, own]

    @pl.when(has_down)
    def _():
        for copy in edge_copies(0):
            copy.wait_recv()
        at = pl.ds(rows, halo)
        field_out[at] = field[at]
        region_out[at] = region[at]
        source_out[:, at] = source[:, at]

    @pl.when(has_up)
    def _():
        for copy in edge_copies(1):
            copy.wait_recv()
        at = pl.ds(up_base, halo)
        field_out[at] = field[at]
        region_out[at] = region[at]
        source_out[:, at] = source[:, at]

    @pl.when(has_up)
    def _():
        for copy in edge_copies(0):
            copy.wait_send()

    @pl.when(has_down)
    def _():
        for copy in edge_copies(1):
            copy.wait_send()


def kernel(
    slices, strips, rows, cols, up_base, total_rows,
    begin, region, source, front_ref,
    ends_out,
    field, coef_a, coef_b, drive,
    decay_own, decay_all, offset_own, offset_all,
    prod_own, prod_all, shift_own, shift_all, solved, end_own, end_prev,
    group_send, group_recv, level_send, level_recv,
    back_send, back_recv, halo_send, halo_recv, end_send, end_recv,
):
    t, x, level, g, levels = grid(slices)
    slab = rows // GROUP
    has_up = x > 0
    has_down = x < strips - 1
    halo = FINE
    groups = total_rows // TILE
    halves = cols // LANES

    def peer(j):
        return level * GROUP + (g + j) % GROUP

    def far(i):
        return ((level + i) % levels) * GROUP + g

    def remote(src, dst, send, recv, tm, space=None):
        return send_to(src, dst, send, recv, tm, x if space is None else space)

    barrier = pltpu.get_barrier_semaphore()

    def greet(tm, space):
        pl.semaphore_signal(
            barrier, inc=1, device_id={"tm": tm, "space": space}, device_id_type=MESH
        )

    expected = (GROUP - 1) + (levels - 1) + 2

    for i in range(1, levels):
        greet(far(i), x)
    greet((t + 1) % slices, x)
    greet((t + slices - 1) % slices, x)

    @pl.when(has_up)
    def _():
        for j in range(GROUP):
            greet(peer(j), x - 1)

    @pl.when(has_down)
    def _():
        for j in range(GROUP):
            greet(peer(j), x + 1)

    for j in range(1, GROUP):
        greet(peer(j), x)

    own = pl.ds(0, rows)
    cos0, sin0 = jnp.float32(1.0), jnp.float32(0.0)
    for b in range(max(1, (slices - 1).bit_length())):
        on = (t // (1 << b)) % 2 == 1
        angle = 2.0 * math.pi * (1 << b) / slices
        cb = jnp.where(on, jnp.float32(math.cos(angle)), jnp.float32(1.0))
        sb = jnp.where(on, jnp.float32(math.sin(angle)), jnp.float32(0.0))
        cos0, sin0 = cos0 * cb - sin0 * sb, sin0 * cb + cos0 * sb
    cos_d = math.cos(2.0 * math.pi / (slices * FINE))
    sin_d = math.sin(2.0 * math.pi / (slices * FINE))
    cut = lax.rem(front_ref[0] + (slices - 1), slices)
    keep = jnp.where(t == cut, jnp.float32(0.0), jnp.float32(1.0))

    count = expected + GROUP * (has_up.astype(jnp.int32) + has_down.astype(jnp.int32))
    sub = lax.broadcasted_iota(jnp.int32, (TILE, LANES), 0)
    lane = lax.broadcasted_iota(jnp.int32, (TILE, LANES), 1)
    top, bottom = sub == 0, sub == TILE - 1
    left, right = lane == 0, lane == LANES - 1
    own_groups = rows // TILE

    def neighbours(v):
        down_roll = [[pltpu.roll(a, 1, 0) for a in line] for line in v]
        up_roll = [[pltpu.roll(a, TILE - 1, 0) for a in line] for line in v]
        right_roll = [[pltpu.roll(a, 1, 1) for a in line] for line in v]
        left_roll = [[pltpu.roll(a, LANES - 1, 1) for a in line] for line in v]
        out = []
        for r in range(groups):
            line = []
            for h in range(halves):
                above = down_roll[r - 1][h]
                if r == 0:
                    above = jnp.where(has_up, above, 0.0)
                below = up_roll[(r + 1) % groups][h]
                if r == own_groups - 1:
                    below = jnp.where(has_down, below, 0.0)
                before = right_roll[r][h - 1] if h > 0 else 0.0
                after = left_roll[r][h + 1] if h < halves - 1 else 0.0
                line.append((
                    jnp.where(top, above, down_roll[r][h]),
                    jnp.where(bottom, below, up_roll[r][h]),
                    jnp.where(left, before, right_roll[r][h]),
                    jnp.where(right, after, left_roll[r][h]),
                ))
            out.append(line)
        return out

    def place(r, h):
        return pl.ds(r * TILE, TILE), pl.ds(h * LANES, LANES)

    def tiles(ref, count):
        return [[ref[place(r, h)] for h in range(halves)] for r in range(count)]

    codes = tiles(region, groups)
    relu = [[lookup(c, RELUCTIVITY) for c in line] for line in codes]
    satu = [[lookup(c, SATURATION) for c in line] for line in codes]
    relu_near, satu_near = neighbours(relu), neighbours(satu)
    for r in range(groups):
        for h in range(halves):
            mobile = lookup(codes[r][h], MOBILITY)
            at = place(r, h)
            for f in range(4):
                face_rel = 0.5 * (relu[r][h] + relu_near[r][h][f])
                face_sat = 0.5 * (satu[r][h] + satu_near[r][h][f])
                base = mobile * face_rel
                coef_b[f, *at] = base * face_sat
                coef_a[f, *at] = base + base * face_sat
            drive[0, *at] = mobile * source[0, *at]
            drive[1, *at] = mobile * source[1, *at]

    def step(v, cos_k, sin_k):
        near = neighbours(v)
        out, diagonals = [], []
        for r in range(groups):
            line, diag_line = [], []
            for h in range(halves):
                at = place(r, h)
                c = v[r][h]
                gain = drive[0, *at] * cos_k + drive[1, *at] * sin_k
                diagonal = None
                for f in range(4):
                    d = near[r][h][f] - c
                    q = coef_a[f, *at] - coef_b[f, *at] * inverse(1.0 + d * d)
                    gain = gain + q * d
                    diagonal = q if diagonal is None else diagonal + q
                line.append(c + gain)
                diag_line.append(diagonal)
            out.append(line)
            diagonals.append(diag_line)
        return out, diagonals

    def flat(v):
        return tuple(a for line in v for a in line)

    def nest(v):
        return [list(v[r * halves:(r + 1) * halves]) for r in range(groups)]

    mine = pl.ds(pl.multiple_of(g * slab, slab), slab)

    def group_copies(it, kind, src, dst):
        out = []
        for j in (2, 3, 1):
            to = (g + j) % GROUP
            out.append(remote(
                src.at[it, pl.ds(pl.multiple_of(to * slab, slab), slab)], dst.at[it, g],
                group_send.at[it, kind], group_recv.at[it, kind], peer(j),
            ))
        return out

    def group_all(it, kind, dst):
        part = dst.at[it, pl.ds(0, GROUP - 1)]
        return remote(part, part, group_send.at[it, kind], group_recv.at[it, kind], peer(1))

    def level_copies(it, kind, src, dst):
        return [
            remote(
                src.at[it], dst.at[it, levels - i - 1],
                level_send.at[it, kind], level_recv.at[it, kind], far(i),
            )
            for i in range(levels - 1, 0, -1)
        ]

    def level_all(it, kind, dst):
        part = dst.at[it]
        return remote(part, part, level_send.at[it, kind], level_recv.at[it, kind], far(1))

    def back_copies(it):
        return [
            remote(
                solved.at[it, (g + j) % GROUP], field.at[it + 1, mine],
                back_send.at[it], back_recv.at[it], peer(j),
            )
            for j in (2, 3, 1)
        ]

    def back_all(it):
        part = solved.at[it, pl.ds(0, GROUP - 1)]
        return remote(part, part, back_send.at[it], back_recv.at[it], peer(1))

    per_halo = halo // slab
    low = g < per_halo
    high = g >= GROUP - per_halo

    def halo_copies(it, way):
        if way == 0:
            start, to = rows + g * slab, x - 1
        else:
            start, to = up_base + (g - (GROUP - per_halo)) * slab, x + 1
        dst = pl.ds(pl.multiple_of(start, slab), slab)
        return [
            remote(
                solved.at[it, (g + j) % GROUP], field.at[it + 1, dst],
                halo_send.at[it, way], halo_recv.at[it, way], peer(j), to,
            )
            for j in (2, 3, 1, 0)
        ]

    def halo_sent(it, way):
        part = solved.at[it]
        return remote(part, part, halo_send.at[it, way], halo_recv.at[it, way], peer(1))

    def halo_here(it, way):
        part = field.at[it + 1, pl.ds(rows if way == 0 else up_base, halo)]
        return remote(part, part, halo_send.at[it, way], halo_recv.at[it, way], peer(1))

    def start_all(copies):
        for copy in copies:
            copy.start()

    def end_copy():
        return remote(end_own, end_prev, end_send, end_recv, (t + 1) % slices)

    for r in range(groups):
        for h in range(halves):
            field[0, *place(r, h)] = begin[place(r, h)]

    def sweep(it, _):
        more = it < ITERS - 1

        def turn(k, carry):
            v, cos_k, sin_k = carry
            v, diagonals = step(nest(v), cos_k, sin_k)
            for _ in range(1, PAIR):
                cos_k, sin_k = cos_k * cos_d - sin_k * sin_d, sin_k * cos_d + cos_k * sin_d
                v, _ = step(v, cos_k, sin_k)

            @pl.when(k == 0)
            def _():
                for r in range(own_groups):
                    for h in range(halves):
                        decay_own[it, *place(r, h)] = keep / (1.0 + FINE * diagonals[r][h])

            @pl.when((it == 0) & (k == DECAY_AT))
            def _():
                pl.semaphore_wait(barrier, count)

            @pl.when(k == DECAY_AT)
            def _():
                start_all(group_copies(it, 0, decay_own, decay_all))
                decay_all[it, g] = decay_own[it, mine]

            @pl.when(k == PRODUCT_AT)
            def _():
                group_all(it, 0, decay_all).wait_recv()
                product = decay_all[it, 0]
                for j in range(1, GROUP):
                    product = product * decay_all[it, j]
                prod_own[it] = product
                start_all(level_copies(it, 0, prod_own, prod_all))

            return flat(v), cos_k * cos_d - sin_k * sin_d, sin_k * cos_d + cos_k * sin_d

        v, _, _ = lax.fori_loop(0, FINE // PAIR, turn, (flat(tiles(field.at[it], groups)), cos0, sin0))
        v = nest(v)
        for r in range(own_groups):
            for h in range(halves):
                at = place(r, h)
                offset_own[it, *at] = v[r][h] - decay_own[it, *at] * field[it, *at]
                end_own[at] = v[r][h]
        start_all(group_copies(it, 1, offset_own, offset_all))
        offset_all[it, g] = offset_own[it, mine]

        @pl.when(jnp.logical_not(more))
        def _():
            end_copy().start()

        group_all(it, 1, offset_all).wait_recv()
        shift = offset_all[it, 0]
        for k in range(1, GROUP):
            shift = decay_all[it, k] * shift + offset_all[it, k]
        shift_own[it] = shift
        start_all(level_copies(it, 1, shift_own, shift_all))
        level_all(it, 0, prod_all).wait_recv()
        level_all(it, 1, shift_all).wait_recv()
        value = shift
        for r in range(levels - 1):
            value = prod_all[it, r] * value + shift_all[it, r]
        solved[it, 0] = value
        for k in range(1, GROUP):
            value = decay_all[it, k - 1] * value + offset_all[it, k - 1]
            solved[it, k] = value
        @pl.when(more & low & has_up)
        def _():
            start_all(halo_copies(it, 0))

        @pl.when(more & high & has_down)
        def _():
            start_all(halo_copies(it, 1))

        start_all(back_copies(it))
        field[it + 1, mine] = solved[it, g]
        back_all(it).wait_recv()

        @pl.when(more & has_down)
        def _():
            halo_here(it, 0).wait_recv()

        @pl.when(more & has_up)
        def _():
            halo_here(it, 1).wait_recv()

        return 0

    lax.fori_loop(0, ITERS, sweep, 0)

    ends_out[0] = field[ITERS, own]
    end_copy().wait_recv()
    ends_out[1] = end_prev[...]
    end_copy().wait_send()

    def settle(it, _):
        more = it < ITERS - 1
        group_all(it, 0, decay_all).wait_send()
        group_all(it, 1, offset_all).wait_send()
        level_all(it, 0, prod_all).wait_send()
        level_all(it, 1, shift_all).wait_send()
        back_all(it).wait_send()

        @pl.when(more & low & has_up)
        def _():
            halo_sent(it, 0).wait_send()

        @pl.when(more & high & has_down)
        def _():
            halo_sent(it, 1).wait_send()

        return 0

    lax.fori_loop(0, ITERS, settle, 0)


def solution(mesh):
    slices, strips = mesh.shape["tm"], mesh.shape["space"]

    def on_device(start_states, region_map, source, front):
        _, rows, cols = start_states.shape
        slab = rows // GROUP
        levels = slices // GROUP
        up_base = rows if strips <= 2 else rows + FINE
        total_rows = up_base + FINE
        f32 = jnp.float32
        dma = pltpu.SemaphoreType.DMA
        vmem = pl.BlockSpec(memory_space=pltpu.VMEM)
        shapes = [
            ((total_rows, cols), f32),
            ((total_rows, cols), jnp.int32),
            ((2, total_rows, cols), f32),
        ]
        wide = pl.pallas_call(
            functools.partial(edge_kernel, strips, rows, up_base),
            out_shape=[jax.ShapeDtypeStruct(*shape) for shape in shapes],
            in_specs=[pl.BlockSpec(memory_space=pltpu.HBM)] * 3,
            out_specs=[vmem] * 3,
            scratch_shapes=[pltpu.VMEM(*shape) for shape in shapes]
            + [dma((3,)), dma((2, 3)), dma((2, 3))],
            compiler_params=pltpu.CompilerParams(
                collective_id=0, has_side_effects=True, vmem_limit_bytes=16 * 2**20
            ),
        )(*(
            pltpu.with_memory_space_constraint(a, pltpu.HBM)
            for a in (start_states, region_map, source)
        ))
        ends = pl.pallas_call(
            functools.partial(kernel, slices, strips, rows, cols, up_base, total_rows),
            out_shape=jax.ShapeDtypeStruct((2, rows, cols), f32),
            in_specs=[vmem] * 3 + [pl.BlockSpec(memory_space=pltpu.SMEM)],
            out_specs=vmem,
            scratch_shapes=[
                pltpu.VMEM((ITERS + 1, total_rows, cols), f32),
                pltpu.VMEM((4, total_rows, cols), f32),
                pltpu.VMEM((4, total_rows, cols), f32),
                pltpu.VMEM((2, total_rows, cols), f32),
                pltpu.VMEM((ITERS, rows, cols), f32),
                pltpu.VMEM((ITERS, GROUP, slab, cols), f32),
                pltpu.VMEM((ITERS, rows, cols), f32),
                pltpu.VMEM((ITERS, GROUP, slab, cols), f32),
                pltpu.VMEM((ITERS, slab, cols), f32),
                pltpu.VMEM((ITERS, levels - 1, slab, cols), f32),
                pltpu.VMEM((ITERS, slab, cols), f32),
                pltpu.VMEM((ITERS, levels - 1, slab, cols), f32),
                pltpu.VMEM((ITERS, GROUP, slab, cols), f32),
                pltpu.VMEM((rows, cols), f32),
                pltpu.VMEM((rows, cols), f32),
                dma((ITERS, 2)),
                dma((ITERS, 2)),
                dma((ITERS, 2)),
                dma((ITERS, 2)),
                dma((ITERS,)),
                dma((ITERS,)),
                dma((ITERS, 2)),
                dma((ITERS, 2)),
                dma,
                dma,
            ],
            compiler_params=pltpu.CompilerParams(
                collective_id=1, has_side_effects=True, vmem_limit_bytes=16 * 2**20
            ),
        )(*wide, jnp.reshape(front, (1,)))
        return ends[0:1], ends[1:2] - ends[0:1]

    placed = (P("tm", "space", None), P("space", None), P(None, "space", None), P())
    return jax.shard_map(
        on_device,
        mesh=mesh,
        in_specs=placed,
        out_specs=(P("tm", "space", None), P("tm", "space", None)),
        check_vma=False,
    )
```
